32 devices in a mesh: rep: 4 (over z), ep: 8 (over y, x, core).
Axes of the slice: x: 2, y: 2, z: 4, core: 2. Of those that a mesh axis runs over, the one named last changes fastest.
Arguments:
- hidden_in: bfloat16 [4096, 2048], P(('rep', 'ep')), may hold values from -3 to 3
- tree_queries: bfloat16 [4096, 2048], P(('rep', 'ep')), may hold values from -6 to 6
- tree_keys: bfloat16 [4096, 2048], P(('rep', 'ep')), may hold values from -6 to 6
- tree_values: bfloat16 [4096, 2048], P(('rep', 'ep')), may hold values from -12 to 12
- tree_parents: int32 [64, 64], P(('rep', 'ep')), may hold values from -1 to 62, as said below
- accepted_nodes: int32 [64, 16], P(('rep', 'ep')), may hold values from 0 to 63
- request_prompt: int32 [64], P(('rep', 'ep')), may hold values from 0 to 3
- prompt_lengths: int32 [16], P('rep'), may hold values from 24 to 192, as said below
- prompt_keys: bfloat16 [16, 192, 2048], P('rep', 'ep'), may hold values from -6 to 6
- prompt_values: bfloat16 [16, 192, 2048], P('rep', 'ep'), may hold values from -12 to 12
- out_proj: bfloat16 [2048, 2048], P('rep'), may hold values from -0.125 to 0.125
- norm_gain: float32 [2048], replicated, may hold values from 0.1 to 1.9
- expert_ids: int32 [4096, 8], P(('rep', 'ep')), may hold values from 0 to 31, all different within a row; in each aligned block of 128 rows (0 to 127, 128 to 255, ...) at most 40 rows name the same one
- gate_weights: float32 [4096, 8], P(('rep', 'ep')), may hold values from 0.05 to 0.5
- expert_gate_up: bfloat16 [32, 2048, 1024], P('ep'), may hold values from -0.125 to 0.125
- expert_down: bfloat16 [32, 512, 2048], P('ep'), may hold values from -0.25 to 0.25
Outputs:
- layer_out: bfloat16 [4096, 2048], P(('rep', 'ep'))
- accepted_cache: bfloat16 [64, 16, 4096], P(('rep', 'ep'))
The draws below stay inside these ranges and needn't reach their ends.
Inputs may be any that keep to these rules, and one draw needn't show every extreme that they name: `tree_parents`: node 0 of every request has parent -1; every other node's parent is one of the 8 nodes before it. `request_prompt`: index of the request's prompt among the 4 prompts of its index of rep. `prompt_lengths`: among the 4 prompts of each index of rep, one has all 192 positions. `expert_ids`: each row names 8 different experts; on the rows of one device no expert is named by more than 40 rows.
All inputs are finite; a program needn't handle non-finite values.
Results may differ from the reference program's by a relative error of at most 0.012.
Values may be sent and summed in bfloat16 or wider, within the bound.
No kernel may reach another device: no remote copies, remote signals or barrier semaphores. Data moves between devices by JAX's collectives and lax.ppermute only.
A program may use at most 128 MiB of HBM per device.

```python
import math
import jax
import jax.numpy as jnp
import numpy as np
from jax import lax

D = 2048
HEADS = 16
HEAD_DIM = 128
TOP = 8
EXPERTS = 32
FF_WIN = 512
TREE = 64
PLEN = 192
PROMPTS = 4
CAP = 40
PATH = 16
TOK_DEV = 128
REQ_ROW = 16
REQUESTS = 64
TOKENS = 4096
GROUPS = 16
N_REP = 4
N_EP = 8


def tree_links(key):
    link_key = jax.random.fold_in(key, 3)
    node_ids = jnp.arange(TREE, dtype=jnp.int32)
    spread = jnp.minimum(jnp.maximum(node_ids, 1), 8)
    random_bits = jax.random.randint(link_key, (REQUESTS, TREE), 0, 65536, dtype=jnp.int32)
    parents = node_ids[None, :] - 1 - random_bits % spread[None, :]
    return jnp.where(node_ids[None, :] == 0, -1, parents).astype(jnp.int32)


def draw_tree_parents(key, part):
    return tree_links(key)


def draw_tree_queries(key, part):
    drawn_rows = jnp.clip(jax.random.normal(jax.random.fold_in(key, 21), (TOKENS, D), jnp.float32), -5.0, 5.0)
    return drawn_rows.astype(jnp.bfloat16)


def draw_tree_keys(key, part):
    drawn_rows = jnp.clip(jax.random.normal(jax.random.fold_in(key, 23), (TOKENS, D), jnp.float32), -5.0, 5.0)
    return drawn_rows.astype(jnp.bfloat16)


def draw_prompt_lengths(key, part):
    rows_count = GROUPS // PROMPTS
    drawn_lengths = jax.random.randint(jax.random.fold_in(key, 5), (rows_count, PROMPTS), PLEN // 8, PLEN + 1, dtype=jnp.int32)
    longest = jax.random.randint(jax.random.fold_in(key, 6), (rows_count, 1), 0, PROMPTS, dtype=jnp.int32)
    drawn_lengths = jnp.where(jnp.arange(PROMPTS, dtype=jnp.int32)[None, :] == longest, PLEN, drawn_lengths)
    return drawn_lengths.reshape(-1).astype(jnp.int32)


def set_ends(values, stream_key, low, largest):
    longest = values.shape.index(max(values.shape))
    spots = []
    for shift in (0, 1):
        where = [jax.random.randint(jax.random.fold_in(stream_key, axis), (), 0, length) for axis, length in enumerate(values.shape)]
        where[longest] = (where[longest] + shift) % values.shape[longest]
        spots.append(tuple(where))
    return values.at[spots[0]].set(low).at[spots[1]].set(largest)


def shard_levels(key, extent, pieces, low, largest):
    def one(position, shards_of):
        draws = jax.random.uniform(jax.random.fold_in(jax.random.fold_in(key, 6), position), (shards_of,), jnp.float32, low / len(pieces), largest / len(pieces))
        return jnp.repeat(jnp.exp(draws), extent[position] // shards_of).reshape((-1,) + (1,) * (len(extent) - position - 1))

    level = one(*pieces[0])
    for cut in pieces[1:]:
        level = level * one(*cut)
    return level


def assign_block(rng, own, number, rows, number_of, top, reach, lean):
    ranking = jax.random.permutation(rng, number_of)
    packed, usual = shares(number_of, rows * top, reach, lean, True), shares(number_of, rows * top, reach, lean, False)
    places = jnp.arange(number_of)

    def named(lengths, turn):
        used = int((lengths > 0).sum())
        fixed = max(1, used // 4)
        shifted = fixed + (places - fixed + turn * (used - fixed)) % max(1, number_of - fixed)
        return jnp.zeros((number_of,), jnp.int32).at[ranking[jnp.where(places < fixed, places, shifted)]].set(jnp.asarray(lengths, jnp.int32))

    lengths = jnp.where(number % 4 == 0, named(packed, number // 4), named(usual, number - number // 4 - 1))
    mixed = jax.random.permutation(jax.random.fold_in(own, 3), number_of)
    source_of, receiver = mixed[0:number_of // 2 * 2:2], mixed[1:number_of // 2 * 2:2]
    slack = jnp.minimum(lengths[source_of] - 1, reach - lengths[receiver]) // 2
    slack = jnp.where((source_of == ranking[0]) | (receiver == ranking[0]) | (lengths[receiver] == 0), 0, jnp.maximum(slack, 0))
    shifted = jax.random.randint(jax.random.fold_in(own, 4), (number_of // 2,), 0, 1 << 20) % (slack + 1)
    lengths = lengths.at[source_of].add(-shifted).at[receiver].add(shifted)
    members = jnp.searchsorted(jnp.cumsum(lengths), jnp.arange(rows * top), side="right").astype(jnp.int32)
    grid = members.reshape(top, rows).T
    grid = grid[jax.random.permutation(jax.random.fold_in(own, 1), rows)]
    turn = jax.random.randint(jax.random.fold_in(own, 2), (rows, 1), 0, top)
    return jnp.take_along_axis(grid, (jnp.arange(top)[None, :] + turn) % top, axis=1)


def shares(count, total, limit, lean, full):
    portions = [(1 << 20) // math.isqrt(rank ** lean) + 1 for rank in range(1, count + 1)]
    largest = limit if full else min(limit, max(-(-total // count), total * portions[0] // sum(portions)))
    least = 1 if total - largest >= count - 1 else 0
    holding, surplus = [largest] + [least] * (count - 1), total - largest - least * (count - 1)
    while surplus > 0:
        candidates = [i for i in range(1, count) if holding[i] < largest] or [i for i in range(1, count) if holding[i] < limit]
        pool, budget = sum([portions[i] for i in candidates]), surplus
        for i in candidates:
            more = min(limit - holding[i], max(1, budget * portions[i] // pool), surplus)
            holding[i] = holding[i] + more
            surplus = surplus - more
    return np.array(holding)


def noise(own_key, extent, deviation, limit, shards=(), kind=jnp.bfloat16):
    result = deviation * jax.random.normal(own_key, extent, jnp.float32)
    if shards:
        result = result * shard_levels(own_key, extent, shards, -0.22, 0.18)
    return jnp.clip(result, -limit, limit).astype(kind)


def setup_inputs(seed: int = 0) -> dict:
    streams_of = jax.random.split(jax.random.key(seed), 17)
    hidden_in = noise(streams_of[0], (TOKENS, D), 0.5, 3.0, ((0, 32),))
    tree_queries = draw_tree_queries(jax.random.fold_in(streams_of[16], 71), 0)
    tree_keys = draw_tree_keys(jax.random.fold_in(streams_of[16], 71), 0)
    tree_values = noise(streams_of[3], (TOKENS, D), 2.0, 12.0, ((0, 32),))
    tree_parents = draw_tree_parents(jax.random.fold_in(streams_of[16], 71), 0)
    accepted_nodes = set_ends(jax.random.randint(streams_of[5], (REQUESTS, PATH), 0, TREE), jax.random.fold_in(streams_of[5], 1), 0, TREE - 1).astype(jnp.int32)
    request_prompt = set_ends(jax.random.randint(streams_of[6], (REQUESTS,), 0, PROMPTS), jax.random.fold_in(streams_of[6], 1), 0, PROMPTS - 1).astype(jnp.int32)
    prompt_lengths = draw_prompt_lengths(jax.random.fold_in(streams_of[16], 71), 0)
    prompt_keys = noise(streams_of[8], (GROUPS, PLEN, D), 1.0, 6.0, ((0, 4), (1, 8)))
    prompt_values = noise(streams_of[9], (GROUPS, PLEN, D), 2.0, 12.0, ((0, 4), (1, 8)))
    out_proj = noise(streams_of[10], (D, D), D ** -0.5, 0.125, ((0, 4),))
    norm_gain = jnp.clip(1.0 + 0.18 * jax.random.normal(streams_of[11], (D,), jnp.float32), 0.1, 1.9)
    expert_ids_keys = jax.random.split(jax.random.fold_in(streams_of[12], 1), TOKENS // TOK_DEV)
    expert_ids_turns = jax.random.permutation(jax.random.fold_in(streams_of[12], 3), TOKENS // TOK_DEV)
    expert_ids = jax.vmap(lambda own, number: assign_block(jax.random.fold_in(streams_of[12], 2), own, number, TOK_DEV, EXPERTS, TOP, CAP, 2))(expert_ids_keys, expert_ids_turns).reshape((TOKENS, TOP))
    gate_weights = jnp.clip(jnp.exp(math.log(0.5) - 2.3025851 * jax.random.uniform(streams_of[13], (TOKENS, TOP), jnp.float32) ** shard_levels(streams_of[13], (TOKENS, TOP), ((0, 32),), -0.2, 0.2)), 0.05, 0.5)
    expert_gate_up = noise(streams_of[14], (EXPERTS, D, 2 * FF_WIN), D ** -0.5, 0.125, ((0, 8),))
    expert_down = noise(streams_of[15], (EXPERTS, FF_WIN, D), FF_WIN ** -0.5, 0.25, ((0, 8),))
    return {"hidden_in": hidden_in, "tree_queries": tree_queries, "tree_keys": tree_keys, "tree_values": tree_values, "tree_parents": tree_parents, "accepted_nodes": accepted_nodes, "request_prompt": request_prompt, "prompt_lengths": prompt_lengths, "prompt_keys": prompt_keys, "prompt_values": prompt_values, "out_proj": out_proj, "norm_gain": norm_gain, "expert_ids": expert_ids, "gate_weights": gate_weights, "expert_gate_up": expert_gate_up, "expert_down": expert_down}


NEG_FILL = -1e+30
EPSILON = 1e-05

def ancestry(parents):
    tree_width = parents.shape[-1]
    node_ids = jnp.arange(tree_width, dtype=jnp.int32)
    linked = jnp.logical_or(parents[..., :, None] == node_ids[None, :], node_ids[:, None] == node_ids[None, :])
    closure = linked.astype(jnp.float32)
    for repeat in range(tree_width.bit_length()):
        closure = jnp.minimum(1.0, jnp.einsum('rij,rjk->rik', closure, closure, precision=lax.Precision.HIGHEST))
    return closure > 0.5

def attend_all(tree_queries, tree_keys, tree_values, tree_parents, request_prompt, prompt_lengths, prompt_keys, prompt_values):
    score_scale = 1.0 / math.sqrt(HEAD_DIM)
    block_size = math.gcd(REQUESTS, 8)

    def one_request(request):
        first_row = request * TREE
        queries = lax.dynamic_slice_in_dim(tree_queries, first_row, TREE, 0).astype(jnp.float32).reshape(TREE, HEADS, HEAD_DIM)
        own_keys = lax.dynamic_slice_in_dim(tree_keys, first_row, TREE, 0).astype(jnp.float32)
        own_values = lax.dynamic_slice_in_dim(tree_values, first_row, TREE, 0).astype(jnp.float32)
        group_index = request // REQ_ROW * PROMPTS + request_prompt[request]
        all_keys = jnp.concatenate([prompt_keys[group_index].astype(jnp.float32), own_keys], axis=0).reshape(PLEN + TREE, HEADS, HEAD_DIM)
        all_values = jnp.concatenate([prompt_values[group_index].astype(jnp.float32), own_values], axis=0).reshape(PLEN + TREE, HEADS, HEAD_DIM)
        tree_seen = ancestry(tree_parents[request][None, :])[0]
        cached_seen = jnp.arange(PLEN, dtype=jnp.int32) < prompt_lengths[group_index]
        visible = jnp.concatenate([jnp.broadcast_to(cached_seen[None, :], (TREE, PLEN)), tree_seen], axis=1)
        scores = jnp.einsum('thd,khd->htk', queries, all_keys) * score_scale
        masked = jnp.where(visible[None], scores, NEG_FILL)
        highest = lax.optimization_barrier(jnp.max(masked, axis=-1, keepdims=True))
        exp_weights = jnp.where(visible[None], jnp.exp(masked - highest), 0.0)
        denominator = lax.optimization_barrier(jnp.sum(exp_weights, axis=-1))
        rounded = lax.optimization_barrier(exp_weights.astype(jnp.bfloat16)).astype(jnp.float32)
        mixed_out = jnp.einsum('htk,khd->thd', rounded, all_values) / jnp.transpose(denominator)[:, :, None]
        return mixed_out.reshape(TREE, D).astype(jnp.bfloat16)
    request_ids = jnp.arange(REQUESTS, dtype=jnp.int32).reshape(REQUESTS // block_size, block_size)
    attended = lax.map(jax.vmap(one_request), request_ids)
    return attended.reshape(TOKENS, D)

def experts_all(normed, expert_ids, gate_weights, expert_gate_up, expert_down):
    flat_ids = expert_ids.reshape(-1)
    ordering = jnp.argsort(flat_ids, stable=True).astype(jnp.int32)
    counts = lax.optimization_barrier(jnp.sum((flat_ids[:, None] == jnp.arange(EXPERTS, dtype=jnp.int32)[None, :]).astype(jnp.int32), axis=0))
    starts = (jnp.cumsum(counts) - counts).astype(jnp.int32)
    row_bound = CAP * N_REP * N_EP
    padded = jnp.concatenate([ordering, jnp.zeros((row_bound,), jnp.int32)])
    flat_gates = gate_weights.reshape(-1)
    hidden_units = expert_down.shape[1]

    def visit(accumulated, expert):
        picked = lax.dynamic_slice_in_dim(padded, starts[expert], row_bound, 0)
        is_valid = jnp.arange(row_bound, dtype=jnp.int32) < counts[expert]
        token_rows = picked // TOP
        inputs = normed[token_rows]
        joint_proj = jnp.dot(inputs, expert_gate_up[expert], preferred_element_type=jnp.float32)
        activated = (jax.nn.silu(joint_proj[:, :hidden_units]) * joint_proj[:, hidden_units:]).astype(jnp.bfloat16)
        produced = jnp.dot(activated, expert_down[expert], preferred_element_type=jnp.float32).astype(jnp.bfloat16)
        weighted = jnp.where(is_valid[:, None], flat_gates[picked][:, None] * produced.astype(jnp.float32), 0.0)
        return (accumulated.at[token_rows].add(weighted), None)
    mixture, unused = lax.scan(visit, jnp.zeros((TOKENS, D), jnp.float32), jnp.arange(EXPERTS, dtype=jnp.int32))
    return mixture

def reference(hidden_in, tree_queries, tree_keys, tree_values, tree_parents, accepted_nodes, request_prompt, prompt_lengths, prompt_keys, prompt_values, out_proj, norm_gain, expert_ids, gate_weights, expert_gate_up, expert_down):
    attended = attend_all(tree_queries, tree_keys, tree_values, tree_parents, request_prompt, prompt_lengths, prompt_keys, prompt_values)
    projected = jnp.dot(attended, out_proj, preferred_element_type=jnp.float32)
    residual = hidden_in.astype(jnp.float32) + projected
    normed = (residual * lax.rsqrt(lax.optimization_barrier(jnp.mean(residual * residual, axis=-1, keepdims=True)) + EPSILON) * norm_gain).astype(jnp.bfloat16)
    mixture = experts_all(normed, expert_ids, gate_weights, expert_gate_up, expert_down)
    layer_out = (residual + mixture).astype(jnp.bfloat16)
    accepted_rows = jnp.arange(REQUESTS, dtype=jnp.int32)[:, None] * TREE + accepted_nodes
    accepted_cache = jnp.concatenate([tree_keys[accepted_rows], tree_values[accepted_rows]], axis=-1)
    return (layer_out, accepted_cache)
```

```python
import math

import jax
import jax.numpy as jnp
from jax import lax
from jax.experimental import pallas as pl
from jax.experimental.pallas import tpu as pltpu
from jax.sharding import PartitionSpec as P

HEADS = 16
HEAD_DIM = 128
CAP = 40

NEG_FILL = -1e30
EPSILON = 1e-05
VMEM_LIMIT = 56 * 1024 * 1024

F32 = jnp.float32
BF16 = jnp.bfloat16


def ancestry(parents):
    tree_width = parents.shape[-1]
    node_ids = jnp.arange(tree_width, dtype=jnp.int32)
    linked = jnp.logical_or(
        parents[..., :, None] == node_ids[None, :], node_ids[:, None] == node_ids[None, :]
    )
    closure = linked.astype(F32)
    for repeat in range(tree_width.bit_length()):
        closure = jnp.minimum(1.0, jnp.einsum("rij,rjk->rik", closure, closure))
    return closure > 0.5


def flip(value, bits, size):
    return lax.ppermute(value, "ep", [(i, i ^ bits) for i in range(size)])


def gather_halves(first, second):
    x_first, y_second = flip(first, 2, 8), flip(second, 4, 8)
    x_second, y_first = flip(second, 2, 8), flip(first, 4, 8)
    s_first, s_second = flip(first, 1, 8), flip(second, 1, 8)
    d_first, d_second = flip(x_first, 4, 8), flip(y_second, 2, 8)
    mine = [(first, second), (x_first, x_second), (y_first, y_second), (d_first, d_second)]
    blocks = []
    for index, pair in enumerate(mine):
        other = (s_first, s_second) if index == 0 else tuple(flip(half, 1, 8) for half in pair)
        blocks += [pair, other]
    return blocks


def attention_body(key_count, *refs):
    queries, tree_keys, tree_values, prompt_bias, tree_bias, accepted = refs[:6]
    keys, values = refs[6 : 6 + key_count], refs[6 + key_count : 6 + 2 * key_count]
    attended, cache, bias = refs[6 + 2 * key_count :]
    rows, features = queries.shape
    prompt_rows = prompt_bias.shape[1]
    request_rows = rows // prompt_bias.shape[0]
    for request in range(prompt_bias.shape[0]):
        bias[request * request_rows : (request + 1) * request_rows, :prompt_rows] = jnp.broadcast_to(
            prompt_bias[request : request + 1, :], (request_rows, prompt_rows)
        )
    bias[:, prompt_rows:] = tree_bias[...]
    scale = 1.0 / math.sqrt(HEAD_DIM)
    for head in range(features // HEAD_DIM):
        lanes = slice(head * HEAD_DIM, (head + 1) * HEAD_DIM)
        all_keys = jnp.concatenate([ref[:, lanes] for ref in keys] + [tree_keys[:, lanes]], axis=0)
        all_values = jnp.concatenate([ref[:, lanes] for ref in values] + [tree_values[:, lanes]], axis=0)
        scores = lax.dot_general(
            queries[:, lanes], all_keys, (((1,), (1,)), ((), ())), preferred_element_type=F32
        )
        scores = scores * scale + bias[...]
        weights = jnp.exp(scores - jnp.max(scores, axis=-1, keepdims=True))
        total = jnp.sum(weights, axis=-1, keepdims=True)
        mixed = jnp.dot(weights.astype(BF16), all_values, preferred_element_type=F32)
        attended[head] = (mixed / total).astype(BF16)
    chosen = accepted[...] == lax.broadcasted_iota(jnp.int32, (accepted.shape[0], rows), 1)
    chosen = jnp.where(chosen, 1.0, 0.0).astype(BF16)
    cache[:, :features] = jnp.dot(chosen, tree_keys[...], preferred_element_type=F32).astype(BF16)
    cache[:, features:] = jnp.dot(chosen, tree_values[...], preferred_element_type=F32).astype(BF16)


def attention(queries, tree_keys, tree_values, prompt_bias, tree_bias, accepted, keys, values):
    rows, features = queries.shape
    heads = features // HEAD_DIM
    width = prompt_bias.shape[1] + rows
    return pl.pallas_call(
        lambda *refs: attention_body(len(keys), *refs),
        out_shape=(
            jax.ShapeDtypeStruct((heads, rows, HEAD_DIM), BF16),
            jax.ShapeDtypeStruct((accepted.shape[0], 2 * features), BF16),
        ),
        scratch_shapes=[pltpu.VMEM((rows, width), F32)],
        compiler_params=pltpu.CompilerParams(vmem_limit_bytes=VMEM_LIMIT),
        cost_estimate=pl.CostEstimate(
            flops=4 * rows * width * features, bytes_accessed=8 * 2**20, transcendentals=heads * rows * width
        ),
        name="attention",
    )(queries, tree_keys, tree_values, prompt_bias, tree_bias, accepted, *keys, *values)


def project_body(layout, head_order, attended, hidden, gain, *refs):
    weights = refs[: len(refs) - 4]
    residual, normed_first, normed_second, ordered = refs[len(refs) - 4 :]
    rows, features = hidden.shape
    for index in range(features // HEAD_DIM):
        ordered[:, index * HEAD_DIM : (index + 1) * HEAD_DIM] = attended[head_order[index]]
    step = 256
    squares = jnp.zeros((rows, 1), F32)
    for column in range(0, features, step):
        pieces = []
        for parts in layout:
            for ref_index, low, high in parts:
                if low <= column < high:
                    pieces.append(weights[ref_index][:, column - low : column - low + step])
        joined = jnp.concatenate(pieces, axis=0)
        total = jnp.dot(ordered[...], joined, preferred_element_type=F32)
        total = total + hidden[:, column : column + step].astype(F32)
        residual[:, column : column + step] = total
        squares = squares + jnp.sum(total * total, axis=-1, keepdims=True)
    factor = lax.rsqrt(squares / features + EPSILON)
    half = rows // 2
    normed_first[...] = (residual[:half, :] * factor[:half] * gain[...]).astype(BF16)
    normed_second[...] = (residual[half:, :] * factor[half:] * gain[...]).astype(BF16)


def project(head_order, attended, hidden, gain, weights, layout):
    rows, features = hidden.shape
    whole = pl.BlockSpec(memory_space=pltpu.VMEM)
    return pl.pallas_call(
        lambda *refs: project_body(layout, *refs),
        out_shape=(
            jax.ShapeDtypeStruct((rows, features), F32),
            jax.ShapeDtypeStruct((rows // 2, features), BF16),
            jax.ShapeDtypeStruct((rows // 2, features), BF16),
        ),
        in_specs=[pl.BlockSpec(memory_space=pltpu.SMEM)] + [whole] * (3 + len(weights)),
        out_specs=(whole,) * 3,
        scratch_shapes=[pltpu.VMEM((rows, features), BF16)],
        compiler_params=pltpu.CompilerParams(vmem_limit_bytes=VMEM_LIMIT),
        cost_estimate=pl.CostEstimate(
            flops=2 * rows * features * features, bytes_accessed=10 * 2**20, transcendentals=0
        ),
        name="project",
    )(head_order, attended, hidden, gain, *weights)


def fetch_projection(out_proj):
    shard_rows, features = out_proj.shape
    heads_here = shard_rows // HEAD_DIM
    me, core = lax.axis_index("rep"), lax.axis_index("ep")
    parity = (core // 2 + core // 4) % 2
    quarter = 2 * parity + core % 2
    far = 2 * (1 - parity) + core % 2
    block = lax.dynamic_slice_in_dim(out_proj, quarter * HEAD_DIM, HEAD_DIM, 0)
    up1 = lax.ppermute(block, "rep", [(0, 1), (1, 2), (2, 3)])
    down1 = lax.ppermute(block, "rep", [(1, 0), (2, 1), (3, 2)])
    up2 = lax.ppermute(up1, "rep", [(1, 2), (2, 3)])
    down2 = lax.ppermute(down1, "rep", [(1, 0), (2, 1)])
    up3 = lax.ppermute(up2, "rep", [(2, 3)])
    down3 = lax.ppermute(down2, "rep", [(1, 0)])
    came = [
        jnp.where(me == 0, down1, up1),
        jnp.where(me == 0, down2, jnp.where(me == 3, up2, down1)),
        jnp.where(me == 0, down3, jnp.where(me == 1, down2, jnp.where(me == 2, up2, up3))),
    ]
    shards = [
        jnp.where(me == 0, 1, me - 1),
        jnp.where(me == 0, 2, jnp.where(me == 3, 1, me + 1)),
        jnp.where(me == 0, 3, jnp.where(me == 1, 3, 0)),
    ]
    half = features // 2
    weights, layout = [out_proj], [[(0, 0, features)]]
    order = [me * heads_here + i for i in range(heads_here)]
    for arrived, shard in zip(came, shards):
        left, right = flip(arrived[:, :half], 2, 8), flip(arrived[:, half:], 4, 8)
        first = len(weights)
        weights += [arrived, flip(arrived, 1, 8), left, right, flip(left, 1, 8), flip(right, 1, 8)]
        layout += [
            [(first, 0, features)],
            [(first + 1, 0, features)],
            [(first + 2, 0, half), (first + 3, half, features)],
            [(first + 4, 0, half), (first + 5, half, features)],
        ]
        base = shard * heads_here
        order += [base + quarter, base + (quarter ^ 1), base + far, base + (far ^ 1)]
    return weights, layout, jnp.stack(order).astype(jnp.int32)


def experts_body(source_count, per_pair, first_expert, ids, gates, gate_up_hbm, down_hbm, *refs):
    sources = refs[:source_count]
    same_core, other_core = refs[source_count : source_count + 2]
    gate_up, down, picked, produced, hidden, chosen, slot_gates, sems = refs[source_count + 2 :]
    local_experts, features, _ = gate_up.shape
    units = down.shape[1]
    pairs, top, tokens = ids.shape
    slots = 2 * CAP
    copies = []
    for expert in range(local_experts):
        copies.append(
            (
                pltpu.make_async_copy(gate_up_hbm.at[expert], gate_up.at[expert], sems.at[0, expert]),
                pltpu.make_async_copy(down_hbm.at[expert], down.at[expert], sems.at[1, expert]),
            )
        )
        copies[-1][0].start()
        copies[-1][1].start()
    earlier = lax.broadcasted_iota(jnp.int32, (tokens, tokens), 0)
    later = lax.broadcasted_iota(jnp.int32, (tokens, tokens), 1)
    before = jnp.where(earlier < later, 1.0, 0.0).astype(BF16)
    slot_ids = lax.broadcasted_iota(jnp.int32, (slots, tokens), 0).astype(F32)
    for pair in range(pairs):
        hits, shares = [], []
        for expert in range(local_experts):
            match = ids[pair] == first_expert[0] + expert
            hits.append(jnp.max(jnp.where(match, 1.0, 0.0), axis=0, keepdims=True))
            shares.append(jnp.sum(jnp.where(match, gates[pair], 0.0), axis=0, keepdims=True))
        stacked = jnp.concatenate(hits + [jnp.zeros((16 - local_experts, tokens), F32)], axis=0)
        places = jnp.dot(stacked.astype(BF16), before, preferred_element_type=F32)
        for expert in range(local_experts):
            place = jnp.where(hits[expert] > 0.5, places[expert : expert + 1], -1.0)
            taken = jnp.where(slot_ids == place, 1.0, 0.0)
            chosen[pair, expert * slots : (expert + 1) * slots, :] = taken.astype(BF16)
            slot_gates[expert, pair * slots : (pair + 1) * slots, :] = jnp.sum(
                taken * shares[expert], axis=1, keepdims=True
            )
        group = sources[pair * per_pair : (pair + 1) * per_pair]
        step = 512
        for column in range(0, features, step):
            rows = jnp.concatenate([ref[:, column : column + step] for ref in group], axis=0)
            for expert in range(local_experts):
                picked[expert, pair * slots : (pair + 1) * slots, column : column + step] = jnp.dot(
                    chosen[pair, expert * slots : (expert + 1) * slots, :], rows, preferred_element_type=F32
                ).astype(BF16)
    chunk = slots * min(pairs, 4)
    for expert in range(local_experts):
        copies[expert][0].wait()
        for low in range(0, pairs * slots, chunk):
            rows = picked[expert, low : low + chunk, :]
            gate_rows = slot_gates[expert, low : low + chunk, :]
            for column in range(0, units, 256):
                gate = jnp.dot(rows, gate_up[expert, :, column : column + 256], preferred_element_type=F32)
                up = jnp.dot(
                    rows, gate_up[expert, :, units + column : units + column + 256], preferred_element_type=F32
                )
                active = gate / (1.0 + jnp.exp(-gate)) * up * gate_rows
                hidden[low : low + chunk, column : column + 256] = active.astype(BF16)
        copies[expert][1].wait()
        for low in range(0, pairs * slots, chunk):
            for column in range(0, features, 512):
                result = jnp.dot(
                    hidden[low : low + chunk, :], down[expert, :, column : column + 512], preferred_element_type=F32
                ).astype(BF16)
                for inner in range(chunk // slots):
                    produced[
                        low // slots + inner, expert * slots : (expert + 1) * slots, column : column + 512
                    ] = result[inner * slots : (inner + 1) * slots]
    for pair in range(pairs):
        for column in range(0, features, 512):
            mixture = lax.dot_general(
                chosen[pair], produced[pair, :, column : column + 512], (((0,), (0,)), ((), ())),
                preferred_element_type=F32,
            ).astype(BF16)
            same_core[pair, :, column : column + 512] = mixture[: tokens // 2]
            other_core[pair, :, column : column + 512] = mixture[tokens // 2 :]


def experts(first_expert, ids, gates, gate_up, down, sources, per_pair):
    pairs, top, tokens = ids.shape
    local_experts, features, _ = gate_up.shape
    units = down.shape[1]
    slots = 2 * CAP
    whole = pl.BlockSpec(memory_space=pltpu.VMEM)
    hbm = pl.BlockSpec(memory_space=pl.ANY)
    return pl.pallas_call(
        lambda *refs: experts_body(len(sources), per_pair, *refs),
        out_shape=(jax.ShapeDtypeStruct((pairs, tokens // 2, features), BF16),) * 2,
        in_specs=[pl.BlockSpec(memory_space=pltpu.SMEM), whole, whole, hbm, hbm] + [whole] * len(sources),
        out_specs=(whole, whole),
        scratch_shapes=[
            pltpu.VMEM(gate_up.shape, BF16),
            pltpu.VMEM(down.shape, BF16),
            pltpu.VMEM((local_experts, pairs * slots, features), BF16),
            pltpu.VMEM((pairs, local_experts * slots, features), BF16),
            pltpu.VMEM((pairs * slots, units), BF16),
            pltpu.VMEM((pairs, local_experts * slots, tokens), BF16),
            pltpu.VMEM((local_experts, pairs * slots, 1), F32),
            pltpu.SemaphoreType.DMA((2, local_experts)),
        ],
        compiler_params=pltpu.CompilerParams(vmem_limit_bytes=VMEM_LIMIT),
        cost_estimate=pl.CostEstimate(
            flops=6 * local_experts * pairs * slots * features * units, bytes_accessed=32 * 2**20, transcendentals=0
        ),
        name="experts",
    )(first_expert, ids, gates, gate_up, down, *sources)


def add_rows(left, right):
    return (left.astype(F32) + right.astype(F32)).astype(BF16)


def return_sums(same_core, other_core):
    swapped = flip(other_core, 1, 8)
    near_x, near_y, across = [add_rows(same_core[g], swapped[g]) for g in (1, 2, 3)]
    half = near_x.shape[0] // 2
    across_first, across_second = flip(across[:half], 2, 8), flip(across[half:], 4, 8)
    x_first, y_second = flip(near_x[:half], 2, 8), flip(near_y[half:], 4, 8)
    x_second = flip(add_rows(near_x[half:], across_second), 2, 8)
    y_first = flip(add_rows(near_y[:half], across_first), 4, 8)
    return [
        same_core[0].astype(F32),
        swapped[0].astype(F32),
        jnp.concatenate([x_first, x_second], axis=0).astype(F32),
        jnp.concatenate([y_first, y_second], axis=0).astype(F32),
    ]


def per_device(
    hidden_in,
    tree_queries,
    tree_keys,
    tree_values,
    tree_parents,
    accepted_nodes,
    request_prompt,
    prompt_lengths,
    prompt_keys,
    prompt_values,
    out_proj,
    norm_gain,
    expert_ids,
    gate_weights,
    expert_gate_up,
    expert_down,
):
    tok_rows, features = hidden_in.shape
    req_count, tree_len = tree_parents.shape
    prompt_count, rows_here, _ = prompt_keys.shape
    top_count = expert_ids.shape[1]
    local_experts = expert_gate_up.shape[0]
    ep_size, rep_size = lax.axis_size("ep"), lax.axis_size("rep")
    me = lax.axis_index("ep")
    planes = ep_size == 8

    if planes:
        flat = (prompt_count * rows_here, features)
        blocks = gather_halves(prompt_keys.reshape(flat), prompt_values.reshape(flat))
        keys, values = [block[0] for block in blocks], [block[1] for block in blocks]
        source = me ^ jnp.arange(ep_size, dtype=jnp.int32)
        position = source[:, None, None] * rows_here + jnp.arange(rows_here, dtype=jnp.int32)[None, None, :]
        shape = (ep_size, prompt_count, rows_here)
        position = jnp.broadcast_to(position, shape).reshape(-1)
        prompt = jnp.broadcast_to(jnp.arange(prompt_count, dtype=jnp.int32)[None, :, None], shape).reshape(-1)
    else:
        all_rows = rows_here * ep_size
        keys = [lax.all_gather(prompt_keys, "ep", axis=1, tiled=True).reshape(-1, features)]
        values = [lax.all_gather(prompt_values, "ep", axis=1, tiled=True).reshape(-1, features)]
        position = jnp.tile(jnp.arange(all_rows, dtype=jnp.int32), prompt_count)
        prompt = jnp.repeat(jnp.arange(prompt_count, dtype=jnp.int32), all_rows)
    request_length = prompt_lengths[request_prompt]
    in_prompt = (prompt[None, :] == request_prompt[:, None]) & (position[None, :] < request_length[:, None])
    prompt_bias = jnp.where(in_prompt, 0.0, NEG_FILL).astype(F32)

    if planes and rep_size == 4 and out_proj.shape[0] == 4 * HEAD_DIM:
        proj_weights, proj_layout, head_order = fetch_projection(out_proj)
    else:
        proj_weights = [lax.all_gather(out_proj, "rep", axis=0, tiled=True)]
        proj_layout = [[(0, 0, features)]]
        head_order = jnp.arange(features // HEAD_DIM, dtype=jnp.int32)

    routing = jnp.concatenate([expert_ids.astype(F32).T, gate_weights.T], axis=0)
    routing = lax.all_gather(routing, "ep", axis=0)
    if planes:
        routing = routing[source]
    routing = routing.reshape(ep_size // 2, 2, 2 * top_count, tok_rows)
    routing = jnp.concatenate([routing[:, 0], routing[:, 1]], axis=-1)
    all_ids, all_gates = routing[:, :top_count].astype(jnp.int32), routing[:, top_count:]

    tree_seen = ancestry(tree_parents)
    same_request = jnp.eye(req_count, dtype=jnp.bool_)
    tree_visible = (tree_seen[:, :, None, :] & same_request[:, None, :, None]).reshape(tok_rows, tok_rows)
    tree_bias = jnp.where(tree_visible, 0.0, NEG_FILL).astype(F32)
    accepted = (jnp.arange(req_count, dtype=jnp.int32)[:, None] * tree_len + accepted_nodes).reshape(-1, 1)
    attended, cache = attention(
        tree_queries, tree_keys, tree_values, prompt_bias, tree_bias, accepted, keys, values
    )
    accepted_cache = cache.reshape(req_count, accepted_nodes.shape[1], 2 * features)

    residual, normed_first, normed_second = project(
        head_order, attended, hidden_in, norm_gain.reshape(1, features), proj_weights, proj_layout
    )

    first_expert = (me * local_experts).astype(jnp.int32).reshape(1)
    if planes:
        sources = [half for block in gather_halves(normed_first, normed_second) for half in block]
        per_pair = 4
    else:
        everyone = lax.all_gather(jnp.concatenate([normed_first, normed_second], axis=0), "ep", axis=0, tiled=True)
        sources = [everyone[i * 2 * tok_rows : (i + 1) * 2 * tok_rows] for i in range(ep_size // 2)]
        per_pair = 1
    same_core, other_core = experts(
        first_expert, all_ids, all_gates, expert_gate_up, expert_down, sources, per_pair
    )
    if planes:
        terms = return_sums(same_core, other_core)
    else:
        shares = jnp.stack([same_core, other_core], axis=1).reshape(ep_size, tok_rows, features)
        shares = lax.all_to_all(shares, "ep", split_axis=0, concat_axis=0, tiled=True)
        terms = [jnp.sum(shares.astype(F32), axis=0)]
    layer_out = residual
    for term in terms:
        layer_out = layer_out + term
    return (layer_out.astype(BF16), accepted_cache)


def solution(mesh):
    in_specs = (
        P(("rep", "ep"), None),
        P(("rep", "ep"), None),
        P(("rep", "ep"), None),
        P(("rep", "ep"), None),
        P(("rep", "ep"), None),
        P(("rep", "ep"), None),
        P(("rep", "ep")),
        P("rep"),
        P("rep", "ep", None),
        P("rep", "ep", None),
        P("rep", None),
        P(),
        P(("rep", "ep"), None),
        P(("rep", "ep"), None),
        P("ep", None, None),
        P("ep", None, None),
    )
    out_specs = (P(("rep", "ep"), None), P(("rep", "ep"), None, None))
    return jax.shard_map(
        per_device, mesh=mesh, in_specs=in_specs, out_specs=out_specs, check_vma=False
    )
```

```python
import math

import jax
import jax.numpy as jnp
from jax import lax
from jax.experimental import pallas as pl
from jax.experimental.pallas import tpu as pltpu
from jax.sharding import PartitionSpec as P

HEADS = 16
HEAD_DIM = 128
CAP = 40

NEG_FILL = -1e30
EPSILON = 1e-05
VMEM_LIMIT = 56 * 1024 * 1024

F32 = jnp.float32
BF16 = jnp.bfloat16


def flip(value, bits, size):
    return lax.ppermute(value, "ep", [(i, i ^ bits) for i in range(size)])


def in_hbm(value):
    return pltpu.with_memory_space_constraint(value, pltpu.HBM)


def in_vmem(value):
    return pltpu.with_memory_space_constraint(value, pltpu.VMEM)


def after(value, *done):
    return lax.optimization_barrier((value, done))[0]


def everywhere(shape, dtype):
    return jax.ShapeDtypeStruct(shape, dtype)


IN_VMEM = pl.BlockSpec(memory_space=pltpu.VMEM)
IN_SMEM = pl.BlockSpec(memory_space=pltpu.SMEM)
IN_PLACE = pl.BlockSpec(memory_space=pl.ANY)


def pack_body(core, *refs):
    sources, (ids, gates), (send, send_prompts, mine, prompts), held, sems = refs[:5], refs[5:7], refs[7:11], refs[11:16], refs[16]
    copies = [pltpu.make_async_copy(sources[i], held[i], sems.at[i]) for i in range(5)]
    for copy in copies:
        copy.start()
    for copy in copies:
        copy.wait()
    queries, keys, values, prompt_keys, prompt_values = held
    rows, features = queries.shape
    shards = features // (4 * HEAD_DIM)
    width = 2 * HEAD_DIM
    for shard in range(shards):
        lanes = slice(shard * width, (shard + 1) * width)
        for target, which in ((0, core[0]), (1, 1 - core[0])):
            start = pl.multiple_of(shard * 2 * width + which * width, width)
            low = 0
            for part in (queries, keys, values, prompt_keys, prompt_values):
                high = low + part.shape[0]
                taken = part[:, pl.ds(start, width)]
                if high <= 3 * rows:
                    (mine, send)[target][low:high, lanes] = taken
                else:
                    (prompts, send_prompts)[target][low - 3 * rows : high - 3 * rows, lanes] = taken
                low = high
    top = ids.shape[0]
    high_part = gates[...].astype(BF16)
    low_part = (gates[...] - high_part.astype(F32)).astype(BF16)
    blank = jnp.zeros((top, rows), F32)
    first = jnp.concatenate([ids[...], high_part.astype(F32)], axis=0).astype(BF16)
    second = jnp.concatenate([blank, low_part.astype(F32)], axis=0).astype(BF16)
    base = 2 * prompt_keys.shape[0]
    for target in (send_prompts, prompts):
        target[base : base + 2 * top, :] = jnp.zeros((2 * top, target.shape[1]), BF16)
        target[base : base + 2 * top, :rows] = first
        target[base : base + 2 * top, rows : 2 * rows] = second


def pack(core, queries, keys, values, prompt_keys, prompt_values, ids, gates):
    rows, features = queries.shape
    tail = 2 * prompt_keys.shape[0] + 2 * ids.shape[0]
    return pl.pallas_call(
        pack_body,
        out_shape=(
            everywhere((3 * rows, features // 2), BF16),
            everywhere((tail, features // 2), BF16),
            everywhere((3 * rows, features // 2), BF16),
            everywhere((tail, features // 2), BF16),
        ),
        in_specs=[IN_SMEM] + [IN_PLACE] * 5 + [IN_VMEM] * 2,
        out_specs=(IN_VMEM,) * 4,
        scratch_shapes=[pltpu.VMEM(part.shape, BF16) for part in (queries, keys, values, prompt_keys, prompt_values)]
        + [pltpu.SemaphoreType.DMA((5,))],
        compiler_params=pltpu.CompilerParams(vmem_limit_bytes=12 * 2**20),
        name="pack",
    )(core, *[in_hbm(part) for part in (queries, keys, values, prompt_keys, prompt_values)], ids, gates)


def attend(queries, all_keys, all_values, bias):
    scores = lax.dot_general(queries, all_keys, (((1,), (1,)), ((), ())), preferred_element_type=F32)
    scores = scores * (1.0 / math.sqrt(HEAD_DIM)) + bias
    weights = jnp.exp(scores - jnp.max(scores, axis=-1, keepdims=True))
    total = jnp.sum(weights, axis=-1, keepdims=True)
    mixed = jnp.dot(weights.astype(BF16), all_values, preferred_element_type=F32)
    return (mixed / total).astype(BF16)


def fill_bias(bias, prompt_rows, tree_len, parents, prompts, lengths, prompt_of, position):
    tokens = bias.shape[0]
    for request in range(tokens // tree_len):
        prompt = prompts[request]
        seen = (prompt_of == prompt) & (position < lengths[prompt])
        row = jnp.where(seen, 0.0, NEG_FILL)
        bias[request * tree_len : (request + 1) * tree_len, :prompt_rows] = jnp.broadcast_to(
            row, (tree_len, prompt_rows)
        )
    node = lax.broadcasted_iota(jnp.int32, (tokens, tokens), 0)
    other = lax.broadcasted_iota(jnp.int32, (tokens, tokens), 1)
    reach = jnp.where((other == parents) | (other == node), 1.0, 0.0)
    for _ in range((tree_len - 1).bit_length()):
        reach = reach.astype(BF16)
        reach = jnp.minimum(jnp.dot(reach, reach, preferred_element_type=F32), 1.0)
    bias[:, prompt_rows:] = jnp.where(reach > 0.5, 0.0, NEG_FILL)


def accepted_body(accepted, tree_keys, tree_values, cache):
    rows, features = tree_keys.shape
    chosen = accepted[...] == lax.broadcasted_iota(jnp.int32, (accepted.shape[0], rows), 1)
    chosen = jnp.where(chosen, 1.0, 0.0).astype(BF16)
    cache[:, :features] = jnp.dot(chosen, tree_keys[...], preferred_element_type=F32).astype(BF16)
    cache[:, features:] = jnp.dot(chosen, tree_values[...], preferred_element_type=F32).astype(BF16)


def chip_attention_body(
    me, my_prompts, sibling, lengths, columns, parents, accepted, *refs
):
    copies = [pltpu.make_async_copy(refs[i], refs[17 + i], refs[29].at[i]) for i in range(12)]
    for copy in copies:
        copy.start()
    (attended, cache, ids, gates, bias), (tree_keys, tree_values, mine, got, *holders) = refs[12:17], refs[17:29]
    rows = tree_keys.shape[0]
    requests = my_prompts.shape[0]
    tree_len = rows // requests
    block = (holders[0].shape[0] - 16) // 2
    prompts = [my_prompts[i] for i in range(requests)] + [sibling[requests + i, 0] for i in range(requests)]
    position = (columns[0:1, :] ^ me[0]) * (block // lengths.shape[0]) + columns[2:3, :]
    fill_bias(bias, columns.shape[1], tree_len, parents[...], prompts, lengths, columns[1:2, :], position)
    for copy in copies:
        copy.wait()
    for head in range(mine.shape[1] // HEAD_DIM):
        lanes = slice(head * HEAD_DIM, (head + 1) * HEAD_DIM)
        queries = jnp.concatenate([mine[:rows, lanes], got[:rows, lanes]], axis=0)
        all_keys = jnp.concatenate(
            [ref[:block, lanes] for ref in holders]
            + [mine[rows : 2 * rows, lanes], got[rows : 2 * rows, lanes]],
            axis=0,
        )
        all_values = jnp.concatenate(
            [ref[block : 2 * block, lanes] for ref in holders]
            + [mine[2 * rows :, lanes], got[2 * rows : 3 * rows, lanes]],
            axis=0,
        )
        attended[head] = attend(queries, all_keys, all_values, bias[...])
    accepted_body(accepted, tree_keys, tree_values, cache)
    for index, ref in enumerate(holders):
        first = ref[2 * block :, :rows].astype(F32)
        second = ref[2 * block :, rows : 2 * rows].astype(F32)
        lanes = slice(index % 2 * rows, (index % 2 + 1) * rows)
        ids[index // 2, :, lanes] = first[:8]
        gates[index // 2, :, lanes] = first[8:] + second[8:]


def chip_attention(scalars, columns, parents, accepted, tree_keys, tree_values, blocks):
    rows, features = tree_keys.shape
    width = columns.shape[1] + 2 * rows
    heads = features // HEAD_DIM // 2
    copied = [in_hbm(part) for part in (tree_keys, tree_values, *blocks)]
    return pl.pallas_call(
        chip_attention_body,
        out_shape=(
            everywhere((heads, 2 * rows, HEAD_DIM), BF16),
            everywhere((accepted.shape[0], 2 * features), BF16),
            everywhere((4, 8, 2 * rows), F32),
            everywhere((4, 8, 2 * rows), F32),
        ),
        in_specs=[IN_SMEM] * 4 + [IN_VMEM] * 3 + [IN_PLACE] * len(copied),
        out_specs=(IN_VMEM,) * 4,
        scratch_shapes=[pltpu.VMEM((2 * rows, width), F32)]
        + [pltpu.VMEM(part.shape, BF16) for part in copied]
        + [pltpu.SemaphoreType.DMA((len(copied),))],
        compiler_params=pltpu.CompilerParams(vmem_limit_bytes=14 * 2**20),
        name="attention",
    )(*scalars, columns, parents, accepted, *copied)


def plain_attention_body(
    prompts, lengths, columns, parents, accepted, queries, tree_keys, tree_values, keys, values, attended, cache, bias
):
    rows, features = queries.shape
    tree_len = rows // prompts.shape[0]
    requests = [prompts[i] for i in range(prompts.shape[0])]
    fill_bias(bias, columns.shape[1], tree_len, parents[...], requests, lengths, columns[0:1, :], columns[1:2, :])
    for head in range(features // HEAD_DIM):
        lanes = slice(head * HEAD_DIM, (head + 1) * HEAD_DIM)
        all_keys = jnp.concatenate([keys[:, lanes], tree_keys[:, lanes]], axis=0)
        all_values = jnp.concatenate([values[:, lanes], tree_values[:, lanes]], axis=0)
        attended[:, lanes] = attend(queries[:, lanes], all_keys, all_values, bias[...])
    accepted_body(accepted, tree_keys, tree_values, cache)


def plain_attention(prompts, lengths, columns, parents, accepted, queries, tree_keys, tree_values, keys, values):
    rows, features = queries.shape
    return pl.pallas_call(
        plain_attention_body,
        out_shape=(everywhere((rows, features), BF16), everywhere((accepted.shape[0], 2 * features), BF16)),
        in_specs=[IN_SMEM] * 2 + [IN_VMEM] * 8,
        out_specs=(IN_VMEM,) * 2,
        scratch_shapes=[pltpu.VMEM((rows, columns.shape[1] + rows), F32)],
        compiler_params=pltpu.CompilerParams(vmem_limit_bytes=VMEM_LIMIT),
        name="attention",
    )(prompts, lengths, columns, parents, accepted, queries, tree_keys, tree_values, keys, values)


def fetch_projection(out_proj, packed, before_shared):
    me, place = lax.axis_index("rep"), lax.axis_index("ep")
    core, parity = place % 2, (place // 2 + place // 4) % 2
    block = lax.dynamic_slice_in_dim(out_proj, (2 * core + parity) * HEAD_DIM, HEAD_DIM, 0)
    own = lax.dynamic_slice_in_dim(out_proj, core * 2 * HEAD_DIM, 2 * HEAD_DIM, 0)
    block = after(block, packed)

    def shifted(value, by):
        return lax.ppermute(value, "rep", [(i, (i + by) % 4) for i in range(4)])

    came1, came3 = shifted(block, 1), shifted(block, 3)
    up = lax.ppermute(came1, "rep", [(1, 2), (2, 3)])
    down = lax.ppermute(came3, "rep", [(2, 1), (1, 0)])
    order = [2 * me, 2 * me + 1]
    for by in (1, 3, 2):
        shard = (me + 4 - by) % 4
        order += [2 * shard + parity, 2 * shard + 1 - parity]
    half = HEAD_DIM // 2
    came1, came3 = after((came1, came3), before_shared)
    first = jnp.concatenate([came1[:half], came3[:half]], axis=0)
    second = jnp.concatenate([came1[half:], came3[half:]], axis=0)
    from_x, from_y = flip(first, 2, 8), flip(second, 4, 8)
    weights = [own, first, second, from_x, from_y]
    pieces = [(0, 0, 2 * HEAD_DIM)]
    for low in (0, half):
        pieces += [(index, low, low + half) for index in (1, 2, 3, 4)]
    pieces += [(5, 0, HEAD_DIM), (6, 0, half), (7, 0, half)]
    up, down = after((up, down), from_x, from_y)
    came2 = jnp.where(me >= 2, up, down)
    return weights, pieces, jnp.stack(order).astype(jnp.int32), came2


def chip_project_body(pieces, order, attended, *refs):
    weights, (mine, other, ordered) = refs[: len(refs) - 3], refs[len(refs) - 3 :]
    rows, features = mine.shape
    for index in range(attended.shape[0]):
        ordered[:, index * HEAD_DIM : (index + 1) * HEAD_DIM] = attended[order[index]]
    step = 256
    for column in range(0, features, step):
        joined = jnp.concatenate(
            [weights[ref][low:high, column : column + step] for ref, low, high in pieces], axis=0
        )
        total = jnp.dot(ordered[...], joined, preferred_element_type=F32)
        mine[:, column : column + step] = total[:rows]
        other[:, column : column + step] = total[rows:].astype(BF16)


def chip_project(order, attended, weights, pieces):
    heads, rows, _ = attended.shape
    features = weights[0].shape[1]
    return pl.pallas_call(
        lambda *refs: chip_project_body(pieces, *refs),
        out_shape=(everywhere((rows // 2, features), F32), everywhere((rows // 2, features), BF16)),
        in_specs=[IN_SMEM] + [IN_VMEM] * (1 + len(weights)),
        out_specs=(IN_VMEM,) * 2,
        scratch_shapes=[pltpu.VMEM((rows, heads * HEAD_DIM), BF16)],
        compiler_params=pltpu.CompilerParams(vmem_limit_bytes=14 * 2**20),
        name="project",
    )(order, attended, *weights)


def norm_body(hidden, mine, other, gain, residual, normed):
    total = hidden[...].astype(F32) + mine[...] + other[...].astype(F32)
    residual[...] = total
    factor = lax.rsqrt(jnp.mean(total * total, axis=-1, keepdims=True) + EPSILON)
    normed[...] = (total * factor * gain[...]).astype(BF16)


def norm(hidden, mine, other, gain):
    return pl.pallas_call(
        norm_body,
        out_shape=(everywhere(hidden.shape, F32), everywhere(hidden.shape, BF16)),
        in_specs=[IN_VMEM] * 4,
        out_specs=(IN_VMEM,) * 2,
        compiler_params=pltpu.CompilerParams(vmem_limit_bytes=8 * 2**20),
        name="norm",
    )(hidden, mine, other, gain)


def experts_body(per_pair, first_expert, ids, gates, gate_up_hbm, down_hbm, *refs):
    pairs, top, tokens = ids.shape
    sources = refs[: pairs * per_pair]
    same_core, other_core, picked, produced, hidden, chosen, slot_gates, gate_up, down, sems = refs[pairs * per_pair :]
    local_experts, features, _ = gate_up.shape
    units = down.shape[1]
    copies = [
        (
            pltpu.make_async_copy(gate_up_hbm.at[expert], gate_up.at[expert], sems.at[0, expert]),
            pltpu.make_async_copy(down_hbm.at[expert], down.at[expert], sems.at[1, expert]),
        )
        for expert in range(local_experts)
    ]
    for first, second in copies[:2]:
        first.start()
        second.start()
    slots = 2 * CAP
    earlier = lax.broadcasted_iota(jnp.int32, (tokens, tokens), 0)
    later = lax.broadcasted_iota(jnp.int32, (tokens, tokens), 1)
    before = jnp.where(earlier < later, 1.0, 0.0).astype(BF16)
    slot_ids = lax.broadcasted_iota(jnp.int32, (slots, tokens), 0).astype(F32)
    for pair in range(pairs):
        hits, shares = [], []
        for expert in range(local_experts):
            match = ids[pair] == (first_expert[0] + expert).astype(F32)
            hits.append(jnp.max(jnp.where(match, 1.0, 0.0), axis=0, keepdims=True))
            shares.append(jnp.sum(jnp.where(match, gates[pair], 0.0), axis=0, keepdims=True))
        stacked = jnp.concatenate(hits + [jnp.zeros((16 - local_experts, tokens), F32)], axis=0)
        places = jnp.dot(stacked.astype(BF16), before, preferred_element_type=F32)
        for expert in range(local_experts):
            place = jnp.where(hits[expert] > 0.5, places[expert : expert + 1], -1.0)
            taken = jnp.where(slot_ids == place, 1.0, 0.0)
            chosen[pair, expert * slots : (expert + 1) * slots, :] = taken.astype(BF16)
            slot_gates[expert, pair * slots : (pair + 1) * slots, :] = jnp.sum(
                taken * shares[expert], axis=1, keepdims=True
            )
        group = sources[pair * per_pair : (pair + 1) * per_pair]
        step = 512
        for column in range(0, features, step):
            rows = jnp.concatenate([ref[:, column : column + step] for ref in group], axis=0)
            found = jnp.dot(chosen[pair], rows, preferred_element_type=F32).astype(BF16)
            for expert in range(local_experts):
                picked[expert, pair * slots : (pair + 1) * slots, column : column + step] = found[
                    expert * slots : (expert + 1) * slots
                ]
    chunk = slots * min(pairs, 4)
    for expert in range(local_experts):
        copies[expert][0].wait()
        for later_copy in copies[expert + 2 : expert + 3]:
            later_copy[0].start()
            later_copy[1].start()
        for low in range(0, pairs * slots, chunk):
            rows = picked[expert, low : low + chunk, :]
            gate_rows = slot_gates[expert, low : low + chunk, :]
            for column in range(0, units, 256):
                gate = jnp.dot(rows, gate_up[expert, :, column : column + 256], preferred_element_type=F32)
                up = jnp.dot(
                    rows, gate_up[expert, :, units + column : units + column + 256], preferred_element_type=F32
                )
                active = gate / (1.0 + jnp.exp(-gate)) * up * gate_rows
                hidden[low : low + chunk, column : column + 256] = active.astype(BF16)
            if low == 0:
                copies[expert][1].wait()
            for column in range(0, features, 512):
                result = jnp.dot(
                    hidden[low : low + chunk, :], down[expert, :, column : column + 512], preferred_element_type=F32
                ).astype(BF16)
                for inner in range(chunk // slots):
                    produced[
                        low // slots + inner, expert * slots : (expert + 1) * slots, column : column + 512
                    ] = result[inner * slots : (inner + 1) * slots]
    for pair in range(pairs):
        for column in range(0, features, 512):
            mixture = lax.dot_general(
                chosen[pair], produced[pair, :, column : column + 512], (((0,), (0,)), ((), ())),
                preferred_element_type=F32,
            ).astype(BF16)
            same_core[pair, :, column : column + 512] = mixture[: tokens // 2]
            other_core[pair, :, column : column + 512] = mixture[tokens // 2 :]


def experts(first_expert, ids, gates, gate_up, down, sources, limit):
    pairs, top, tokens = ids.shape
    local_experts, features, _ = gate_up.shape
    units = down.shape[1]
    slots = 2 * CAP
    return pl.pallas_call(
        lambda *refs: experts_body(len(sources) // pairs, *refs),
        out_shape=(everywhere((pairs, tokens // 2, features), BF16),) * 2,
        in_specs=[IN_SMEM] + [IN_VMEM] * 2 + [IN_PLACE] * 2 + [IN_VMEM] * len(sources),
        out_specs=(IN_VMEM,) * 2,
        scratch_shapes=[
            pltpu.VMEM((local_experts, pairs * slots, features), BF16),
            pltpu.VMEM((pairs, local_experts * slots, features), BF16),
            pltpu.VMEM((pairs * slots, units), BF16),
            pltpu.VMEM((pairs, local_experts * slots, tokens), BF16),
            pltpu.VMEM((local_experts, pairs * slots, 1), F32),
            pltpu.VMEM(gate_up.shape, BF16),
            pltpu.VMEM(down.shape, BF16),
            pltpu.SemaphoreType.DMA((2, local_experts)),
        ],
        compiler_params=pltpu.CompilerParams(vmem_limit_bytes=limit),
        name="experts",
    )(first_expert, ids, gates, in_hbm(gate_up), in_hbm(down), *sources)


def add_rows(left, right):
    return (left.astype(F32) + right.astype(F32)).astype(BF16)


def on_planes(
    hidden_in, tree_queries, tree_keys, tree_values, parents, accepted, tree_parents, request_prompt, prompt_lengths,
    prompt_keys, prompt_values, out_proj, gain, expert_ids, gate_weights, gate_up, down,
):
    tok_rows, features = hidden_in.shape
    prompt_count, rows_here, _ = prompt_keys.shape
    me = lax.axis_index("ep").astype(jnp.int32)

    flat = (prompt_count * rows_here, features)
    send, send_prompts, mine, prompts = pack(
        (me % 2).reshape(1), tree_queries, tree_keys, tree_values, prompt_keys.reshape(flat),
        prompt_values.reshape(flat), expert_ids.astype(F32).T, gate_weights.T,
    )
    x_mine, y_mine = flip(prompts, 2, 8), flip(prompts, 4, 8)
    theirs = flip(send_prompts, 1, 8)
    x_theirs, y_theirs = flip(theirs, 2, 8), flip(theirs, 4, 8)
    far_a, far_b = flip(x_mine, 4, 8), flip(y_theirs, 2, 8)
    weights, pieces, order, last = fetch_projection(out_proj, prompts, (x_mine, y_mine, x_theirs, y_theirs, far_a, far_b))
    got = flip(send, 1, 8)
    small = jnp.concatenate(
        [tree_parents, jnp.broadcast_to(request_prompt[:, None], tree_parents.shape)], axis=0
    )
    sibling = flip(small, 1, 8)

    column = jnp.arange(8 * flat[0], dtype=jnp.int32)
    columns = jnp.stack([column // flat[0], column % flat[0] // rows_here, column % rows_here])
    chip_parents = jnp.concatenate([tree_parents, sibling[: tree_parents.shape[0]]], axis=0)
    first_node = jnp.arange(chip_parents.shape[0], dtype=jnp.int32)[:, None] * tree_parents.shape[1]
    chip_parents = jnp.where(chip_parents < 0, -1, chip_parents + first_node).reshape(-1, 1)
    attended, cache, ids, gates = chip_attention(
        (me.reshape(1), request_prompt, sibling, prompt_lengths), columns, chip_parents, accepted,
        tree_keys, tree_values, (mine, got, prompts, theirs, x_mine, x_theirs, y_mine, y_theirs, far_a, far_b),
    )
    last = after(last, attended, *weights[3:5])
    edge = last.shape[0] // 2
    weights += [last, flip(last[:edge], 2, 8), flip(last[edge:], 4, 8)]
    mine, other = chip_project(order, attended, weights, pieces)
    residual, normed = norm(hidden_in, mine, flip(other, 1, 8), gain)

    across = flip(normed, 6, 8)
    sibling_rows = flip(normed, 1, 8)
    first_expert = (me * gate_up.shape[0]).reshape(1)

    def run(low, high, sources, *done):
        limit = (34 + 8 * (high - low)) * 2**20
        return experts(first_expert, after(ids[low:high], done), gates[low:high], gate_up, down, sources, limit)

    near_same, near_other = run(0, 1, [normed, sibling_rows])
    sent, across = after((normed, across), near_same)
    from_x, from_y = flip(sent, 2, 8), flip(sent, 4, 8)
    far_same, far_other = run(3, 4, [across, flip(across, 1, 8)])
    far = add_rows(far_same, flip(after(far_other, from_x, from_y), 1, 8))
    back = flip(far[0], 6, 8)
    from_x, from_y = after((from_x, from_y), far)
    beside = [from_x, flip(from_x, 1, 8), from_y, flip(from_y, 1, 8)]
    side_same, side_other = run(1, 3, beside)
    side = add_rows(side_same, flip(after(side_other, back), 1, 8))
    terms = [near_same[0], flip(near_other, 1, 8)[0], back, flip(side[0], 2, 8), flip(side[1], 4, 8)]
    return residual, terms, cache


def on_any_mesh(
    hidden_in, tree_queries, tree_keys, tree_values, parents, accepted, tree_parents, request_prompt, prompt_lengths,
    prompt_keys, prompt_values, out_proj, gain, expert_ids, gate_weights, gate_up, down,
):
    tok_rows, features = hidden_in.shape
    prompt_count, rows_here, _ = prompt_keys.shape
    ep_size = lax.axis_size("ep")
    me = lax.axis_index("ep").astype(jnp.int32)
    keys = lax.all_gather(prompt_keys, "ep", axis=1, tiled=True).reshape(-1, features)
    values = lax.all_gather(prompt_values, "ep", axis=1, tiled=True).reshape(-1, features)
    column = jnp.arange(keys.shape[0], dtype=jnp.int32)
    columns = jnp.stack([column // (rows_here * ep_size), column % (rows_here * ep_size)])
    attended, cache = plain_attention(
        request_prompt, prompt_lengths, columns, parents, accepted, tree_queries, tree_keys, tree_values, keys, values
    )
    joined = lax.all_gather(out_proj, "rep", axis=0, tiled=True)
    projected = jnp.dot(attended, joined, preferred_element_type=F32)
    residual, normed = norm(hidden_in, projected, jnp.zeros(hidden_in.shape, BF16), gain)
    routing = jnp.concatenate([expert_ids.astype(F32).T, gate_weights.T], axis=0)
    routing = lax.all_gather(routing, "ep", axis=0).reshape(ep_size // 2, 2, -1, tok_rows)
    routing = jnp.concatenate([routing[:, 0], routing[:, 1]], axis=-1)
    top = expert_ids.shape[1]
    everyone = lax.all_gather(normed, "ep", axis=0, tiled=True)
    sources = [everyone[i * 2 * tok_rows : (i + 1) * 2 * tok_rows] for i in range(ep_size // 2)]
    same_core, other_core = experts(
        (me * gate_up.shape[0]).reshape(1), routing[:, :top], routing[:, top:], gate_up, down, sources, VMEM_LIMIT
    )
    shares = jnp.stack([same_core, other_core], axis=1).reshape(ep_size, tok_rows, features)
    shares = lax.all_to_all(shares, "ep", split_axis=0, concat_axis=0, tiled=True)
    return residual, [shares[i] for i in range(ep_size)], cache


def per_device(
    hidden_in,
    tree_queries,
    tree_keys,
    tree_values,
    tree_parents,
    accepted_nodes,
    request_prompt,
    prompt_lengths,
    prompt_keys,
    prompt_values,
    out_proj,
    norm_gain,
    expert_ids,
    gate_weights,
    expert_gate_up,
    expert_down,
):
    tok_rows, features = hidden_in.shape
    req_count, tree_len = tree_parents.shape
    first_node = jnp.arange(req_count, dtype=jnp.int32)[:, None] * tree_len
    accepted = (first_node + accepted_nodes).reshape(-1, 1)
    parents = jnp.where(tree_parents < 0, -1, tree_parents + first_node).reshape(-1, 1)
    planes = lax.axis_size("ep") == 8 and lax.axis_size("rep") == 4 and out_proj.shape[0] == 4 * HEAD_DIM
    plan = on_planes if planes else on_any_mesh
    residual, terms, cache = plan(
        hidden_in, tree_queries, tree_keys, tree_values, parents, accepted, tree_parents, request_prompt,
        prompt_lengths, prompt_keys, prompt_values, out_proj, norm_gain.reshape(1, features), expert_ids,
        gate_weights, expert_gate_up, expert_down,
    )
    layer_out = residual
    for term in terms:
        layer_out = layer_out + term.astype(F32)
    accepted_cache = cache.reshape(req_count, accepted_nodes.shape[1], 2 * features)
    return (layer_out.astype(BF16), accepted_cache)


def solution(mesh):
    in_specs = (
        P(("rep", "ep"), None),
        P(("rep", "ep"), None),
        P(("rep", "ep"), None),
        P(("rep", "ep"), None),
        P(("rep", "ep"), None),
        P(("rep", "ep"), None),
        P(("rep", "ep")),
        P("rep"),
        P("rep", "ep", None),
        P("rep", "ep", None),
        P("rep", None),
        P(),
        P(("rep", "ep"), None),
        P(("rep", "ep"), None),
        P("ep", None, None),
        P("ep", None, None),
    )
    out_specs = (P(("rep", "ep"), None), P(("rep", "ep"), None, None))
    return jax.shard_map(
        per_device, mesh=mesh, in_specs=in_specs, out_specs=out_specs, check_vma=False
    )
```

```python
import math

import jax
import jax.numpy as jnp
from jax import lax
from jax.experimental import pallas as pl
from jax.experimental.pallas import tpu as pltpu
from jax.sharding import PartitionSpec as P

HEADS = 16
HEAD_DIM = 128
CAP = 40

NEG_FILL = -1e30
EPSILON = 1e-05
VMEM_LIMIT = 56 * 1024 * 1024

F32 = jnp.float32
BF16 = jnp.bfloat16


def flip(value, bits, size):
    return lax.ppermute(value, "ep", [(i, i ^ bits) for i in range(size)])


def in_hbm(value):
    return pltpu.with_memory_space_constraint(value, pltpu.HBM)


def in_vmem(value):
    return pltpu.with_memory_space_constraint(value, pltpu.VMEM)


def after(value, *done):
    return lax.optimization_barrier((value, done))[0]


def everywhere(shape, dtype):
    return jax.ShapeDtypeStruct(shape, dtype)


IN_VMEM = pl.BlockSpec(memory_space=pltpu.VMEM)
IN_SMEM = pl.BlockSpec(memory_space=pltpu.SMEM)
IN_PLACE = pl.BlockSpec(memory_space=pl.ANY)


def pack_body(core, *refs):
    sources, (send, send_prompts, mine, prompts), held, sems = refs[:7], refs[7:11], refs[11:18], refs[18]
    copies = [pltpu.make_async_copy(sources[i], held[i], sems.at[i]) for i in range(7)]
    for copy in copies:
        copy.start()
    for copy in copies:
        copy.wait()
    queries, keys, values, prompt_keys, prompt_values, ids, gates = held
    rows, features = queries.shape
    shards = features // (4 * HEAD_DIM)
    width = 2 * HEAD_DIM
    for shard in range(shards):
        lanes = slice(shard * width, (shard + 1) * width)
        for target, which in ((0, core[0]), (1, 1 - core[0])):
            start = pl.multiple_of(shard * 2 * width + which * width, width)
            low = 0
            for part in (queries, keys, values, prompt_keys, prompt_values):
                high = low + part.shape[0]
                taken = part[:, pl.ds(start, width)]
                if high <= 3 * rows:
                    (mine, send)[target][low:high, lanes] = taken
                else:
                    (prompts, send_prompts)[target][low - 3 * rows : high - 3 * rows, lanes] = taken
                low = high
    top = ids.shape[0]
    high_part = gates[...].astype(BF16)
    low_part = (gates[...] - high_part.astype(F32)).astype(BF16)
    blank = jnp.zeros((top, rows), F32)
    first = jnp.concatenate([ids[...].astype(F32), high_part.astype(F32)], axis=0).astype(BF16)
    second = jnp.concatenate([blank, low_part.astype(F32)], axis=0).astype(BF16)
    base = 2 * prompt_keys.shape[0]
    for target in (send_prompts, prompts):
        target[base : base + 2 * top, :] = jnp.zeros((2 * top, target.shape[1]), BF16)
        target[base : base + 2 * top, :rows] = first
        target[base : base + 2 * top, rows : 2 * rows] = second


def pack(core, queries, keys, values, prompt_keys, prompt_values, ids, gates):
    rows, features = queries.shape
    tail = 2 * prompt_keys.shape[0] + 2 * ids.shape[0]
    parts = (queries, keys, values, prompt_keys, prompt_values, ids, gates)
    return pl.pallas_call(
        pack_body,
        out_shape=(
            everywhere((3 * rows, features // 2), BF16),
            everywhere((tail, features // 2), BF16),
            everywhere((3 * rows, features // 2), BF16),
            everywhere((tail, features // 2), BF16),
        ),
        in_specs=[IN_SMEM] + [IN_PLACE] * 7,
        out_specs=(IN_VMEM,) * 4,
        scratch_shapes=[pltpu.VMEM(part.shape, part.dtype) for part in parts] + [pltpu.SemaphoreType.DMA((7,))],
        compiler_params=pltpu.CompilerParams(vmem_limit_bytes=12 * 2**20),
        name="pack",
    )(core, *[in_hbm(part) for part in parts])


def attend(queries, all_keys, all_values, bias):
    scores = lax.dot_general(queries, all_keys, (((1,), (1,)), ((), ())), preferred_element_type=F32)
    scores = scores * (1.0 / math.sqrt(HEAD_DIM)) + bias
    weights = jnp.exp(scores - jnp.max(scores, axis=-1, keepdims=True))
    total = jnp.sum(weights, axis=-1, keepdims=True)
    mixed = jnp.dot(weights.astype(BF16), all_values, preferred_element_type=F32)
    return (mixed / total).astype(BF16)


def fill_bias(bias, prompt_rows, tree_len, parents, prompts, lengths, prompt_of, position):
    tokens = bias.shape[0]
    for request in range(tokens // tree_len):
        prompt = prompts[request]
        seen = (prompt_of == prompt) & (position < lengths[prompt])
        row = jnp.where(seen, 0.0, NEG_FILL)
        bias[request * tree_len : (request + 1) * tree_len, :prompt_rows] = jnp.broadcast_to(
            row, (tree_len, prompt_rows)
        )
    node = lax.broadcasted_iota(jnp.int32, (tokens, tokens), 0)
    other = lax.broadcasted_iota(jnp.int32, (tokens, tokens), 1)
    reach = jnp.where((other == parents) | (other == node), 1.0, 0.0)
    for _ in range((tree_len - 1).bit_length()):
        reach = reach.astype(BF16)
        reach = jnp.minimum(jnp.dot(reach, reach, preferred_element_type=F32), 1.0)
    bias[:, prompt_rows:] = jnp.where(reach > 0.5, 0.0, NEG_FILL)


def accepted_body(accepted, tree_keys, tree_values, cache):
    rows, features = tree_keys.shape
    chosen = accepted[...] == lax.broadcasted_iota(jnp.int32, (accepted.shape[0], rows), 1)
    chosen = jnp.where(chosen, 1.0, 0.0).astype(BF16)
    cache[:, :features] = jnp.dot(chosen, tree_keys[...], preferred_element_type=F32).astype(BF16)
    cache[:, features:] = jnp.dot(chosen, tree_values[...], preferred_element_type=F32).astype(BF16)


def chip_attention_body(
    me, my_prompts, sibling, lengths, columns, parents, accepted, mine, prompts_here, *refs
):
    copies = [pltpu.make_async_copy(refs[i], refs[15 + i], refs[25].at[i]) for i in range(10)]
    for copy in copies:
        copy.start()
    (attended, cache, ids, gates, bias), (tree_keys, tree_values, got, *holders) = refs[10:15], refs[15:25]
    holders = [prompts_here, *holders]
    rows = tree_keys.shape[0]
    requests = my_prompts.shape[0]
    tree_len = rows // requests
    block = (holders[0].shape[0] - 16) // 2
    prompts = [my_prompts[i] for i in range(requests)] + [sibling[requests + i, 0] for i in range(requests)]
    position = (columns[0:1, :] ^ me[0]) * (block // lengths.shape[0]) + columns[2:3, :]
    fill_bias(bias, columns.shape[1], tree_len, parents[...], prompts, lengths, columns[1:2, :], position)
    for copy in copies:
        copy.wait()
    for head in range(mine.shape[1] // HEAD_DIM):
        lanes = slice(head * HEAD_DIM, (head + 1) * HEAD_DIM)
        queries = jnp.concatenate([mine[:rows, lanes], got[:rows, lanes]], axis=0)
        all_keys = jnp.concatenate(
            [ref[:block, lanes] for ref in holders]
            + [mine[rows : 2 * rows, lanes], got[rows : 2 * rows, lanes]],
            axis=0,
        )
        all_values = jnp.concatenate(
            [ref[block : 2 * block, lanes] for ref in holders]
            + [mine[2 * rows :, lanes], got[2 * rows : 3 * rows, lanes]],
            axis=0,
        )
        attended[head] = attend(queries, all_keys, all_values, bias[...])
    accepted_body(accepted, tree_keys, tree_values, cache)
    for index, ref in enumerate(holders):
        first = ref[2 * block :, :rows].astype(F32)
        second = ref[2 * block :, rows : 2 * rows].astype(F32)
        lanes = slice(index % 2 * rows, (index % 2 + 1) * rows)
        ids[index // 2, :, lanes] = first[:8]
        gates[index // 2, :, lanes] = first[8:] + second[8:]


def chip_attention(scalars, columns, parents, accepted, tree_keys, tree_values, mine, prompts, blocks):
    rows, features = tree_keys.shape
    width = columns.shape[1] + 2 * rows
    heads = features // HEAD_DIM // 2
    copied = [in_hbm(part) for part in (tree_keys, tree_values, *blocks)]
    kept = (mine, prompts)
    return pl.pallas_call(
        chip_attention_body,
        out_shape=(
            everywhere((heads, 2 * rows, HEAD_DIM), BF16),
            everywhere((accepted.shape[0], 2 * features), BF16),
            everywhere((4, 8, 2 * rows), F32),
            everywhere((4, 8, 2 * rows), F32),
        ),
        in_specs=[IN_SMEM] * 4 + [IN_VMEM] * 5 + [IN_PLACE] * len(copied),
        out_specs=(IN_VMEM,) * 4,
        scratch_shapes=[pltpu.VMEM((2 * rows, width), F32)]
        + [pltpu.VMEM(part.shape, BF16) for part in copied]
        + [pltpu.SemaphoreType.DMA((len(copied),))],
        compiler_params=pltpu.CompilerParams(vmem_limit_bytes=14 * 2**20),
        name="attention",
    )(*scalars, columns, parents, accepted, *kept, *copied)


def plain_attention_body(
    prompts, lengths, columns, parents, accepted, queries, tree_keys, tree_values, keys, values, attended, cache, bias
):
    rows, features = queries.shape
    tree_len = rows // prompts.shape[0]
    requests = [prompts[i] for i in range(prompts.shape[0])]
    fill_bias(bias, columns.shape[1], tree_len, parents[...], requests, lengths, columns[0:1, :], columns[1:2, :])
    for head in range(features // HEAD_DIM):
        lanes = slice(head * HEAD_DIM, (head + 1) * HEAD_DIM)
        all_keys = jnp.concatenate([keys[:, lanes], tree_keys[:, lanes]], axis=0)
        all_values = jnp.concatenate([values[:, lanes], tree_values[:, lanes]], axis=0)
        attended[:, lanes] = attend(queries[:, lanes], all_keys, all_values, bias[...])
    accepted_body(accepted, tree_keys, tree_values, cache)


def plain_attention(prompts, lengths, columns, parents, accepted, queries, tree_keys, tree_values, keys, values):
    rows, features = queries.shape
    return pl.pallas_call(
        plain_attention_body,
        out_shape=(everywhere((rows, features), BF16), everywhere((accepted.shape[0], 2 * features), BF16)),
        in_specs=[IN_SMEM] * 2 + [IN_VMEM] * 8,
        out_specs=(IN_VMEM,) * 2,
        scratch_shapes=[pltpu.VMEM((rows, columns.shape[1] + rows), F32)],
        compiler_params=pltpu.CompilerParams(vmem_limit_bytes=VMEM_LIMIT),
        name="attention",
    )(prompts, lengths, columns, parents, accepted, queries, tree_keys, tree_values, keys, values)


def fetch_projection(out_proj, packed, before_shared):
    me, place = lax.axis_index("rep"), lax.axis_index("ep")
    core, parity = place % 2, (place // 2 + place // 4) % 2
    block = lax.dynamic_slice_in_dim(out_proj, (2 * core + parity) * HEAD_DIM, HEAD_DIM, 0)
    own = lax.dynamic_slice_in_dim(out_proj, core * 2 * HEAD_DIM, 2 * HEAD_DIM, 0)
    block = after(block, packed)

    def shifted(value, by):
        return lax.ppermute(value, "rep", [(i, (i + by) % 4) for i in range(4)])

    came1, came3 = shifted(block, 1), shifted(block, 3)
    up = lax.ppermute(came1, "rep", [(1, 2), (2, 3)])
    down = lax.ppermute(came3, "rep", [(2, 1), (1, 0)])
    order = [2 * me, 2 * me + 1]
    for by in (1, 3, 2):
        shard = (me + 4 - by) % 4
        order += [2 * shard + parity, 2 * shard + 1 - parity]
    half = HEAD_DIM // 2
    came1, came3 = after((came1, came3), before_shared)
    first = jnp.concatenate([came1[:half], came3[:half]], axis=0)
    second = jnp.concatenate([came1[half:], came3[half:]], axis=0)
    from_x, from_y = flip(first, 2, 8), flip(second, 4, 8)
    weights = [own, first, second, from_x, from_y]
    pieces = [(0, 0, 2 * HEAD_DIM)]
    for low in (0, half):
        pieces += [(index, low, low + half) for index in (1, 2, 3, 4)]
    pieces += [(index, 0, half) for index in (5, 6, 7, 8)]
    return weights, pieces, jnp.stack(order).astype(jnp.int32), up, down


def chip_project_body(pieces, low_row, order, attended, *refs):
    weights, (result, ordered) = refs[: len(refs) - 2], refs[len(refs) - 2 :]
    rows, features = result.shape
    for index in range(attended.shape[0]):
        ordered[:, index * HEAD_DIM : (index + 1) * HEAD_DIM] = attended[order[index], low_row : low_row + rows, :]
    step = 256
    for column in range(0, features, step):
        joined = jnp.concatenate(
            [weights[ref][low:high, column : column + step] for ref, low, high in pieces], axis=0
        )
        total = jnp.dot(ordered[...], joined, preferred_element_type=F32)
        result[:, column : column + step] = total.astype(result.dtype)


def chip_project(order, attended, weights, pieces, low_row, dtype):
    heads, rows, _ = attended.shape
    features = weights[0].shape[1]
    return pl.pallas_call(
        lambda *refs: chip_project_body(pieces, low_row, *refs),
        out_shape=everywhere((rows // 2, features), dtype),
        in_specs=[IN_SMEM] + [IN_VMEM] * (1 + len(weights)),
        out_specs=IN_VMEM,
        scratch_shapes=[pltpu.VMEM((rows // 2, heads * HEAD_DIM), BF16)],
        compiler_params=pltpu.CompilerParams(vmem_limit_bytes=14 * 2**20),
        name="project",
    )(order, attended, *weights)


def norm_body(hidden, mine, other, gain, residual, normed):
    total = hidden[...].astype(F32) + mine[...] + other[...].astype(F32)
    residual[...] = total
    factor = lax.rsqrt(jnp.mean(total * total, axis=-1, keepdims=True) + EPSILON)
    normed[...] = (total * factor * gain[...]).astype(BF16)


def norm(hidden, mine, other, gain):
    return pl.pallas_call(
        norm_body,
        out_shape=(everywhere(hidden.shape, F32), everywhere(hidden.shape, BF16)),
        in_specs=[IN_VMEM] * 4,
        out_specs=(IN_VMEM,) * 2,
        compiler_params=pltpu.CompilerParams(vmem_limit_bytes=8 * 2**20),
        name="norm",
    )(hidden, mine, other, gain)


def stage_body(gate_up, down, *refs):
    count = gate_up.shape[0]
    sems = refs[2 * count]
    copies = []
    for expert in range(count):
        copies.append(pltpu.make_async_copy(gate_up.at[expert], refs[expert], sems.at[expert]))
        copies.append(pltpu.make_async_copy(down.at[expert], refs[count + expert], sems.at[count + expert]))
    for copy in copies:
        copy.start()
    for copy in copies:
        copy.wait()


def stage(gate_up, down):
    count = gate_up.shape[0]
    staged = pl.pallas_call(
        stage_body,
        out_shape=[pltpu.VMEM(gate_up.shape[1:], BF16)] * count + [pltpu.VMEM(down.shape[1:], BF16)] * count,
        in_specs=[IN_PLACE] * 2,
        out_specs=[IN_PLACE] * (2 * count),
        scratch_shapes=[pltpu.SemaphoreType.DMA((2 * count,))],
        compiler_params=pltpu.CompilerParams(vmem_limit_bytes=2**20),
        cost_estimate=pl.CostEstimate(flops=0, bytes_accessed=2 * (gate_up.size + down.size), transcendentals=0),
        name="stage",
    )(in_hbm(gate_up), in_hbm(down))
    return staged[:count], staged[count:]


def experts_body(per_pair, local_experts, first_expert, ids, gates, *refs):
    pairs, top, tokens = ids.shape
    gate_up, down, refs = refs[:local_experts], refs[local_experts : 2 * local_experts], refs[2 * local_experts :]
    sources = refs[: pairs * per_pair]
    same_core, other_core, picked, produced, hidden, chosen, slot_gates = refs[pairs * per_pair :]
    features, units = gate_up[0].shape[0], down[0].shape[0]
    slots = 2 * CAP
    earlier = lax.broadcasted_iota(jnp.int32, (tokens, tokens), 0)
    later = lax.broadcasted_iota(jnp.int32, (tokens, tokens), 1)
    before = jnp.where(earlier < later, 1.0, 0.0).astype(BF16)
    slot_ids = lax.broadcasted_iota(jnp.int32, (slots, tokens), 0).astype(F32)
    for pair in range(pairs):
        hits, shares = [], []
        for expert in range(local_experts):
            match = ids[pair] == (first_expert[0] + expert).astype(F32)
            hits.append(jnp.max(jnp.where(match, 1.0, 0.0), axis=0, keepdims=True))
            shares.append(jnp.sum(jnp.where(match, gates[pair], 0.0), axis=0, keepdims=True))
        stacked = jnp.concatenate(hits + [jnp.zeros((16 - local_experts, tokens), F32)], axis=0)
        places = jnp.dot(stacked.astype(BF16), before, preferred_element_type=F32)
        for expert in range(local_experts):
            place = jnp.where(hits[expert] > 0.5, places[expert : expert + 1], -1.0)
            taken = jnp.where(slot_ids == place, 1.0, 0.0)
            chosen[pair, expert * slots : (expert + 1) * slots, :] = taken.astype(BF16)
            slot_gates[expert, pair * slots : (pair + 1) * slots, :] = jnp.sum(
                taken * shares[expert], axis=1, keepdims=True
            )
        group = sources[pair * per_pair : (pair + 1) * per_pair]
        step = 512
        for column in range(0, features, step):
            rows = jnp.concatenate([ref[:, column : column + step] for ref in group], axis=0)
            found = jnp.dot(chosen[pair], rows, preferred_element_type=F32).astype(BF16)
            for expert in range(local_experts):
                picked[expert, pair * slots : (pair + 1) * slots, column : column + step] = found[
                    expert * slots : (expert + 1) * slots
                ]
    chunk = slots * min(pairs, 4)
    for expert in range(local_experts):
        for low in range(0, pairs * slots, chunk):
            rows = picked[expert, low : low + chunk, :]
            gate_rows = slot_gates[expert, low : low + chunk, :]
            for column in range(0, units, 256):
                gate = jnp.dot(rows, gate_up[expert][:, column : column + 256], preferred_element_type=F32)
                up = jnp.dot(
                    rows, gate_up[expert][:, units + column : units + column + 256], preferred_element_type=F32
                )
                active = gate / (1.0 + jnp.exp(-gate)) * up * gate_rows
                hidden[low : low + chunk, column : column + 256] = active.astype(BF16)
            for column in range(0, features, 512):
                result = jnp.dot(
                    hidden[low : low + chunk, :], down[expert][:, column : column + 512], preferred_element_type=F32
                ).astype(BF16)
                for inner in range(chunk // slots):
                    produced[
                        low // slots + inner, expert * slots : (expert + 1) * slots, column : column + 512
                    ] = result[inner * slots : (inner + 1) * slots]
    for pair in range(pairs):
        for column in range(0, features, 512):
            mixture = lax.dot_general(
                chosen[pair], produced[pair, :, column : column + 512], (((0,), (0,)), ((), ())),
                preferred_element_type=F32,
            ).astype(BF16)
            same_core[pair, :, column : column + 512] = mixture[: tokens // 2]
            other_core[pair, :, column : column + 512] = mixture[tokens // 2 :]


def experts(first_expert, ids, gates, gate_up, down, sources, limit, pin=False):
    pairs, top, tokens = ids.shape
    local_experts, (features, _) = len(gate_up), gate_up[0].shape
    units = down[0].shape[0]
    slots = 2 * CAP
    matrices = [*gate_up, *down]
    if pin:
        matrices = [in_vmem(part) for part in matrices]
    return pl.pallas_call(
        lambda *refs: experts_body(len(sources) // pairs, local_experts, *refs),
        out_shape=(everywhere((pairs, tokens // 2, features), BF16),) * 2,
        in_specs=[IN_SMEM] + [IN_VMEM] * (2 + 2 * local_experts + len(sources)),
        out_specs=(IN_VMEM,) * 2,
        scratch_shapes=[
            pltpu.VMEM((local_experts, pairs * slots, features), BF16),
            pltpu.VMEM((pairs, local_experts * slots, features), BF16),
            pltpu.VMEM((pairs * slots, units), BF16),
            pltpu.VMEM((pairs, local_experts * slots, tokens), BF16),
            pltpu.VMEM((local_experts, pairs * slots, 1), F32),
        ],
        compiler_params=pltpu.CompilerParams(vmem_limit_bytes=limit),
        cost_estimate=pl.CostEstimate(
            flops=12 * local_experts * pairs * slots * features * units, bytes_accessed=16 * 2**20, transcendentals=0
        ),
        name="experts",
    )(first_expert, ids, gates, *matrices, *sources)


def add_rows(left, right):
    return (left.astype(F32) + right.astype(F32)).astype(BF16)


def on_planes(
    hidden_in, tree_queries, tree_keys, tree_values, parents, accepted, tree_parents, request_prompt, prompt_lengths,
    prompt_keys, prompt_values, out_proj, gain, expert_ids, gate_weights, gate_up, down,
):
    tok_rows, features = hidden_in.shape
    prompt_count, rows_here, _ = prompt_keys.shape
    me = lax.axis_index("ep").astype(jnp.int32)

    flat = (prompt_count * rows_here, features)
    send, send_prompts, mine, prompts = pack(
        (me % 2).reshape(1), tree_queries, tree_keys, tree_values, prompt_keys.reshape(flat),
        prompt_values.reshape(flat), expert_ids.T, gate_weights.T,
    )
    x_mine, y_mine = flip(prompts, 2, 8), flip(prompts, 4, 8)
    theirs = flip(send_prompts, 1, 8)
    x_theirs, y_theirs = flip(theirs, 2, 8), flip(theirs, 4, 8)
    far_a, far_b = flip(x_mine, 4, 8), flip(y_theirs, 2, 8)
    weights, pieces, order, up, down_rows = fetch_projection(out_proj, prompts, (x_mine, y_mine, x_theirs, y_theirs, far_a, far_b))
    got = flip(send, 1, 8)
    small = jnp.concatenate(
        [tree_parents, jnp.broadcast_to(request_prompt[:, None], tree_parents.shape)], axis=0
    )
    sibling = flip(small, 1, 8)

    column = jnp.arange(8 * flat[0], dtype=jnp.int32)
    columns = jnp.stack([column // flat[0], column % flat[0] // rows_here, column % rows_here])
    chip_parents = jnp.concatenate([tree_parents, sibling[: tree_parents.shape[0]]], axis=0)
    first_node = jnp.arange(chip_parents.shape[0], dtype=jnp.int32)[:, None] * tree_parents.shape[1]
    chip_parents = jnp.where(chip_parents < 0, -1, chip_parents + first_node).reshape(-1, 1)
    attended, cache, ids, gates = chip_attention(
        (me.reshape(1), request_prompt, sibling, prompt_lengths), columns, chip_parents, accepted,
        tree_keys, tree_values, mine, prompts, (got, theirs, x_mine, x_theirs, y_mine, y_theirs, far_a, far_b),
    )
    up, down_rows = after((up, down_rows), attended)
    edge = up.shape[0] // 2
    last_first, last_second = [
        jnp.where(lax.axis_index("rep") >= 2, up[rows], down_rows[rows]) for rows in (slice(0, edge), slice(edge, None))
    ]
    weights += [last_first, last_second, flip(last_first, 2, 8), flip(last_second, 4, 8)]
    other = flip(chip_project(order, attended, weights, pieces, tok_rows, BF16), 1, 8)
    mine = chip_project(order, attended, weights, pieces, 0, F32)
    residual, normed = norm(hidden_in, mine, other, gain)

    across, from_x, from_y = flip(normed, 6, 8), flip(normed, 2, 8), flip(normed, 4, 8)
    sibling_rows = flip(normed, 1, 8)
    first_expert = (me * gate_up.shape[0]).reshape(1)
    gate_up, down = stage(*after((gate_up, down), normed))

    def run(low, high, sources, megabytes, *done):
        return experts(
            first_expert, after(ids[low:high], done), gates[low:high], gate_up, down, sources, megabytes * 2**20, True
        )

    near_same, near_other = run(0, 1, [normed, sibling_rows], 12)
    across = after(across, near_same)
    far_same, far_other = run(3, 4, [across, flip(across, 1, 8)], 12)
    far = add_rows(far_same, flip(far_other, 1, 8))[0]

    half = tok_rows // 2
    far_first, far_second = flip(far[:half], 2, 8), flip(far[half:], 4, 8)
    beside = [from_x, flip(from_x, 1, 8), from_y, flip(from_y, 1, 8)]
    side_same, side_other = run(1, 3, beside, 16, far)
    side = [part.astype(F32) for part in (side_same, flip(after(side_other, far_first, far_second), 1, 8))]
    side = side[0] + side[1]
    to_x = jnp.concatenate([side[0, :half], side[0, half:] + far_second.astype(F32)], axis=0).astype(BF16)
    to_y = jnp.concatenate([side[1, :half] + far_first.astype(F32), side[1, half:]], axis=0).astype(BF16)
    terms = [near_same[0], flip(near_other, 1, 8)[0], flip(to_x, 2, 8), flip(to_y, 4, 8)]
    return residual, terms, cache


def on_any_mesh(
    hidden_in, tree_queries, tree_keys, tree_values, parents, accepted, tree_parents, request_prompt, prompt_lengths,
    prompt_keys, prompt_values, out_proj, gain, expert_ids, gate_weights, gate_up, down,
):
    tok_rows, features = hidden_in.shape
    prompt_count, rows_here, _ = prompt_keys.shape
    ep_size = lax.axis_size("ep")
    me = lax.axis_index("ep").astype(jnp.int32)
    keys = lax.all_gather(prompt_keys, "ep", axis=1, tiled=True).reshape(-1, features)
    values = lax.all_gather(prompt_values, "ep", axis=1, tiled=True).reshape(-1, features)
    column = jnp.arange(keys.shape[0], dtype=jnp.int32)
    columns = jnp.stack([column // (rows_here * ep_size), column % (rows_here * ep_size)])
    attended, cache = plain_attention(
        request_prompt, prompt_lengths, columns, parents, accepted, tree_queries, tree_keys, tree_values, keys, values
    )
    joined = lax.all_gather(out_proj, "rep", axis=0, tiled=True)
    projected = jnp.dot(attended, joined, preferred_element_type=F32)
    residual, normed = norm(hidden_in, projected, jnp.zeros(hidden_in.shape, BF16), gain)
    routing = jnp.concatenate([expert_ids.astype(F32).T, gate_weights.T], axis=0)
    routing = lax.all_gather(routing, "ep", axis=0).reshape(ep_size // 2, 2, -1, tok_rows)
    routing = jnp.concatenate([routing[:, 0], routing[:, 1]], axis=-1)
    top = expert_ids.shape[1]
    everyone = lax.all_gather(normed, "ep", axis=0, tiled=True)
    sources = [everyone[i * 2 * tok_rows : (i + 1) * 2 * tok_rows] for i in range(ep_size // 2)]
    same_core, other_core = experts(
        (me * gate_up.shape[0]).reshape(1), routing[:, :top], routing[:, top:], list(gate_up), list(down), sources,
        VMEM_LIMIT
    )
    shares = jnp.stack([same_core, other_core], axis=1).reshape(ep_size, tok_rows, features)
    shares = lax.all_to_all(shares, "ep", split_axis=0, concat_axis=0, tiled=True)
    return residual, [shares[i] for i in range(ep_size)], cache


def per_device(
    hidden_in,
    tree_queries,
    tree_keys,
    tree_values,
    tree_parents,
    accepted_nodes,
    request_prompt,
    prompt_lengths,
    prompt_keys,
    prompt_values,
    out_proj,
    norm_gain,
    expert_ids,
    gate_weights,
    expert_gate_up,
    expert_down,
):
    tok_rows, features = hidden_in.shape
    req_count, tree_len = tree_parents.shape
    first_node = jnp.arange(req_count, dtype=jnp.int32)[:, None] * tree_len
    accepted = (first_node + accepted_nodes).reshape(-1, 1)
    parents = jnp.where(tree_parents < 0, -1, tree_parents + first_node).reshape(-1, 1)
    planes = lax.axis_size("ep") == 8 and lax.axis_size("rep") == 4 and out_proj.shape[0] == 4 * HEAD_DIM
    plan = on_planes if planes else on_any_mesh
    residual, terms, cache = plan(
        hidden_in, tree_queries, tree_keys, tree_values, parents, accepted, tree_parents, request_prompt,
        prompt_lengths, prompt_keys, prompt_values, out_proj, norm_gain.reshape(1, features), expert_ids,
        gate_weights, expert_gate_up, expert_down,
    )
    layer_out = residual
    for term in terms:
        layer_out = layer_out + term.astype(F32)
    accepted_cache = cache.reshape(req_count, accepted_nodes.shape[1], 2 * features)
    return (layer_out.astype(BF16), accepted_cache)


def solution(mesh):
    in_specs = (
        P(("rep", "ep"), None),
        P(("rep", "ep"), None),
        P(("rep", "ep"), None),
        P(("rep", "ep"), None),
        P(("rep", "ep"), None),
        P(("rep", "ep"), None),
        P(("rep", "ep")),
        P("rep"),
        P("rep", "ep", None),
        P("rep", "ep", None),
        P("rep", None),
        P(),
        P(("rep", "ep"), None),
        P(("rep", "ep"), None),
        P("ep", None, None),
        P("ep", None, None),
    )
    out_specs = (P(("rep", "ep"), None), P(("rep", "ep"), None, None))
    return jax.shard_map(
        per_device, mesh=mesh, in_specs=in_specs, out_specs=out_specs, check_vma=False
    )
```

```python
import math

import jax
import jax.numpy as jnp
from jax import lax
from jax.experimental import pallas as pl
from jax.experimental.pallas import tpu as pltpu
from jax.sharding import PartitionSpec as P

HEADS = 16
HEAD_DIM = 128
CAP = 40

NEG_FILL = -1e30
EPSILON = 1e-05
VMEM_LIMIT = 56 * 1024 * 1024

F32 = jnp.float32
BF16 = jnp.bfloat16


def flip(value, bits, size):
    return lax.ppermute(value, "ep", [(i, i ^ bits) for i in range(size)])


def in_hbm(value):
    return pltpu.with_memory_space_constraint(value, pltpu.HBM)


def in_vmem(value):
    return pltpu.with_memory_space_constraint(value, pltpu.VMEM)


def after(value, *done):
    return lax.optimization_barrier((value, done))[0]


def everywhere(shape, dtype):
    return jax.ShapeDtypeStruct(shape, dtype)


IN_VMEM = pl.BlockSpec(memory_space=pltpu.VMEM)
IN_SMEM = pl.BlockSpec(memory_space=pltpu.SMEM)
IN_PLACE = pl.BlockSpec(memory_space=pl.ANY)


def pack_body(place, *refs):
    sources, out_proj, (send, send_prompts, prompts, block) = refs[:7], refs[7], refs[8:12]
    held, sems = refs[12:19], refs[19]
    core, parity = place[0] % 2, (place[0] // 2 + place[0] // 4) % 2
    head_rows = pl.ds(pl.multiple_of((2 * core + parity) * HEAD_DIM, HEAD_DIM), HEAD_DIM)
    copies = [pltpu.make_async_copy(sources[i], held[i], sems.at[i]) for i in range(7)]
    copies.append(pltpu.make_async_copy(out_proj.at[head_rows], block, sems.at[7]))
    for copy in copies:
        copy.start()
    for copy in copies:
        copy.wait()
    queries, keys, values, prompt_keys, prompt_values, ids, gates = held
    rows, features = queries.shape
    shards = features // (4 * HEAD_DIM)
    width = 2 * HEAD_DIM
    for shard in range(shards):
        lanes = slice(shard * width, (shard + 1) * width)
        for target, which in ((0, core), (1, 1 - core)):
            start = pl.multiple_of(shard * 2 * width + which * width, width)
            low = 0
            for part in (queries, keys, values, prompt_keys, prompt_values):
                high = low + part.shape[0]
                if high > 3 * rows:
                    kept = slice(low - 3 * rows, high - 3 * rows)
                    (prompts, send_prompts)[target][kept, lanes] = part[:, pl.ds(start, width)]
                elif target == 1:
                    send[low:high, lanes] = part[:, pl.ds(start, width)]
                low = high
    top = ids.shape[0]
    high_part = gates[...].astype(BF16)
    low_part = (gates[...] - high_part.astype(F32)).astype(BF16)
    blank = jnp.zeros((top, rows), F32)
    first = jnp.concatenate([ids[...].astype(F32), high_part.astype(F32)], axis=0).astype(BF16)
    second = jnp.concatenate([blank, low_part.astype(F32)], axis=0).astype(BF16)
    base = 2 * prompt_keys.shape[0]
    for target in (send_prompts, prompts):
        target[base : base + 2 * top, :] = jnp.zeros((2 * top, target.shape[1]), BF16)
        target[base : base + 2 * top, :rows] = first
        target[base : base + 2 * top, rows : 2 * rows] = second


def pack(place, queries, keys, values, prompt_keys, prompt_values, ids, gates, out_proj):
    rows, features = queries.shape
    tail = 2 * prompt_keys.shape[0] + 2 * ids.shape[0]
    parts = (queries, keys, values, prompt_keys, prompt_values, ids, gates)
    return pl.pallas_call(
        pack_body,
        out_shape=(
            everywhere((3 * rows, features // 2), BF16),
            everywhere((tail, features // 2), BF16),
            everywhere((tail, features // 2), BF16),
            everywhere((HEAD_DIM, features), BF16),
        ),
        in_specs=[IN_SMEM] + [IN_PLACE] * 8,
        out_specs=(IN_VMEM,) * 4,
        scratch_shapes=[pltpu.VMEM(part.shape, part.dtype) for part in parts] + [pltpu.SemaphoreType.DMA((8,))],
        compiler_params=pltpu.CompilerParams(vmem_limit_bytes=12 * 2**20),
        name="pack",
    )(place, *[in_hbm(part) for part in (*parts, out_proj)])


def attend(queries, all_keys, all_values, bias):
    scores = lax.dot_general(queries, all_keys, (((1,), (1,)), ((), ())), preferred_element_type=F32)
    scores = scores * (1.0 / math.sqrt(HEAD_DIM)) + bias
    weights = jnp.exp(scores - jnp.max(scores, axis=-1, keepdims=True))
    total = jnp.sum(weights, axis=-1, keepdims=True)
    mixed = jnp.dot(weights.astype(BF16), all_values, preferred_element_type=F32)
    return (mixed / total).astype(BF16)


def fill_bias(bias, prompt_rows, tree_len, parents, prompts, lengths, prompt_of, position):
    tokens = bias.shape[0]
    for request in range(tokens // tree_len):
        prompt = prompts[request]
        seen = (prompt_of == prompt) & (position < lengths[prompt])
        row = jnp.where(seen, 0.0, NEG_FILL)
        bias[request * tree_len : (request + 1) * tree_len, :prompt_rows] = jnp.broadcast_to(
            row, (tree_len, prompt_rows)
        )
    node = lax.broadcasted_iota(jnp.int32, (tokens, tokens), 0)
    other = lax.broadcasted_iota(jnp.int32, (tokens, tokens), 1)
    reach = jnp.where((other == parents) | (other == node), 1.0, 0.0)
    for _ in range((tree_len - 1).bit_length()):
        reach = reach.astype(BF16)
        reach = jnp.minimum(jnp.dot(reach, reach, preferred_element_type=F32), 1.0)
    bias[:, prompt_rows:] = jnp.where(reach > 0.5, 0.0, NEG_FILL)


def accepted_body(accepted, tree_keys, tree_values, cache):
    rows, features = tree_keys.shape
    chosen = accepted[...] == lax.broadcasted_iota(jnp.int32, (accepted.shape[0], rows), 1)
    chosen = jnp.where(chosen, 1.0, 0.0).astype(BF16)
    cache[:, :features] = jnp.dot(chosen, tree_keys[...], preferred_element_type=F32).astype(BF16)
    cache[:, features:] = jnp.dot(chosen, tree_values[...], preferred_element_type=F32).astype(BF16)


def chip_attention_body(
    me, my_prompts, sibling, lengths, columns, parents, accepted, prompts_here, *refs
):
    copies = [pltpu.make_async_copy(refs[i], refs[16 + i], refs[27].at[i]) for i in range(11)]
    for copy in copies:
        copy.start()
    (attended, cache, ids, gates, bias), (queries_here, tree_keys, tree_values, got, *holders) = refs[11:16], refs[16:27]
    holders = [prompts_here, *holders]
    rows = tree_keys.shape[0]
    requests = my_prompts.shape[0]
    tree_len = rows // requests
    block = (holders[0].shape[0] - 16) // 2
    prompts = [my_prompts[i] for i in range(requests)] + [sibling[requests + i, 0] for i in range(requests)]
    position = (columns[0:1, :] ^ me[0]) * (block // lengths.shape[0]) + columns[2:3, :]
    fill_bias(bias, columns.shape[1], tree_len, parents[...], prompts, lengths, columns[1:2, :], position)
    for copy in copies:
        copy.wait()
    for head in range(got.shape[1] // HEAD_DIM):
        lanes = slice(head * HEAD_DIM, (head + 1) * HEAD_DIM)
        place = head // 2 * 4 * HEAD_DIM + me[0] % 2 * 2 * HEAD_DIM + head % 2 * HEAD_DIM
        mine = pl.ds(pl.multiple_of(place, HEAD_DIM), HEAD_DIM)
        queries = jnp.concatenate([queries_here[:, mine], got[:rows, lanes]], axis=0)
        all_keys = jnp.concatenate(
            [ref[:block, lanes] for ref in holders]
            + [tree_keys[:, mine], got[rows : 2 * rows, lanes]],
            axis=0,
        )
        all_values = jnp.concatenate(
            [ref[block : 2 * block, lanes] for ref in holders]
            + [tree_values[:, mine], got[2 * rows : 3 * rows, lanes]],
            axis=0,
        )
        attended[head] = attend(queries, all_keys, all_values, bias[...])
    accepted_body(accepted, tree_keys, tree_values, cache)
    for index, ref in enumerate(holders):
        first = ref[2 * block :, :rows].astype(F32)
        second = ref[2 * block :, rows : 2 * rows].astype(F32)
        lanes = slice(index % 2 * rows, (index % 2 + 1) * rows)
        ids[index // 2, :, lanes] = first[:8]
        gates[index // 2, :, lanes] = first[8:] + second[8:]


def chip_attention(scalars, columns, parents, accepted, queries, tree_keys, tree_values, prompts, blocks):
    rows, features = tree_keys.shape
    width = columns.shape[1] + 2 * rows
    heads = features // HEAD_DIM // 2
    copied = [in_hbm(part) for part in (queries, tree_keys, tree_values, *blocks)]
    return pl.pallas_call(
        chip_attention_body,
        out_shape=(
            everywhere((heads, 2 * rows, HEAD_DIM), BF16),
            everywhere((accepted.shape[0], 2 * features), BF16),
            everywhere((4, 8, 2 * rows), F32),
            everywhere((4, 8, 2 * rows), F32),
        ),
        in_specs=[IN_SMEM] * 4 + [IN_VMEM] * 4 + [IN_PLACE] * len(copied),
        out_specs=(IN_VMEM,) * 4,
        scratch_shapes=[pltpu.VMEM((2 * rows, width), F32)]
        + [pltpu.VMEM(part.shape, BF16) for part in copied]
        + [pltpu.SemaphoreType.DMA((len(copied),))],
        compiler_params=pltpu.CompilerParams(vmem_limit_bytes=14 * 2**20),
        name="attention",
    )(*scalars, columns, parents, accepted, prompts, *copied)


def plain_attention_body(
    prompts, lengths, columns, parents, accepted, queries, tree_keys, tree_values, keys, values, attended, cache, bias
):
    rows, features = queries.shape
    tree_len = rows // prompts.shape[0]
    requests = [prompts[i] for i in range(prompts.shape[0])]
    fill_bias(bias, columns.shape[1], tree_len, parents[...], requests, lengths, columns[0:1, :], columns[1:2, :])
    for head in range(features // HEAD_DIM):
        lanes = slice(head * HEAD_DIM, (head + 1) * HEAD_DIM)
        all_keys = jnp.concatenate([keys[:, lanes], tree_keys[:, lanes]], axis=0)
        all_values = jnp.concatenate([values[:, lanes], tree_values[:, lanes]], axis=0)
        attended[:, lanes] = attend(queries[:, lanes], all_keys, all_values, bias[...])
    accepted_body(accepted, tree_keys, tree_values, cache)


def plain_attention(prompts, lengths, columns, parents, accepted, queries, tree_keys, tree_values, keys, values):
    rows, features = queries.shape
    return pl.pallas_call(
        plain_attention_body,
        out_shape=(everywhere((rows, features), BF16), everywhere((accepted.shape[0], 2 * features), BF16)),
        in_specs=[IN_SMEM] * 2 + [IN_VMEM] * 8,
        out_specs=(IN_VMEM,) * 2,
        scratch_shapes=[pltpu.VMEM((rows, columns.shape[1] + rows), F32)],
        compiler_params=pltpu.CompilerParams(vmem_limit_bytes=VMEM_LIMIT),
        name="attention",
    )(prompts, lengths, columns, parents, accepted, queries, tree_keys, tree_values, keys, values)


def fetch_projection(out_proj, block, before_shared):
    me, place = lax.axis_index("rep"), lax.axis_index("ep")
    core, parity = place % 2, (place // 2 + place // 4) % 2
    own = lax.dynamic_slice_in_dim(out_proj, core * 2 * HEAD_DIM, 2 * HEAD_DIM, 0)

    def shifted(value, by):
        return lax.ppermute(value, "rep", [(i, (i + by) % 4) for i in range(4)])

    came1, came3 = shifted(block, 1), shifted(block, 3)
    up = lax.ppermute(came1, "rep", [(1, 2), (2, 3)])
    down = lax.ppermute(came3, "rep", [(2, 1), (1, 0)])
    order = [2 * me, 2 * me + 1]
    for by in (1, 3, 2):
        shard = (me + 4 - by) % 4
        order += [2 * shard + parity, 2 * shard + 1 - parity]
    half = HEAD_DIM // 2
    came1, came3 = after((came1, came3), before_shared)
    first = jnp.concatenate([came1[:half], came3[:half]], axis=0)
    second = jnp.concatenate([came1[half:], came3[half:]], axis=0)
    from_x, from_y = flip(first, 2, 8), flip(second, 4, 8)
    weights = [own, first, second, from_x, from_y]
    pieces = [(0, 0, 2 * HEAD_DIM)]
    for low in (0, half):
        pieces += [(index, low, low + half) for index in (1, 2, 3, 4)]
    pieces += [(index, 0, half) for index in (5, 6, 7, 8)]
    return weights, pieces, jnp.stack(order).astype(jnp.int32), up, down


def chip_project_body(pieces, low_row, order, attended, *refs):
    weights, (result, ordered) = refs[: len(refs) - 2], refs[len(refs) - 2 :]
    rows, features = result.shape
    for index in range(attended.shape[0]):
        ordered[:, index * HEAD_DIM : (index + 1) * HEAD_DIM] = attended[order[index], low_row : low_row + rows, :]
    step = 256
    for column in range(0, features, step):
        joined = jnp.concatenate(
            [weights[ref][low:high, column : column + step] for ref, low, high in pieces], axis=0
        )
        total = jnp.dot(ordered[...], joined, preferred_element_type=F32)
        result[:, column : column + step] = total.astype(result.dtype)


def chip_project(order, attended, weights, pieces, low_row, dtype):
    heads, rows, _ = attended.shape
    features = weights[0].shape[1]
    return pl.pallas_call(
        lambda *refs: chip_project_body(pieces, low_row, *refs),
        out_shape=everywhere((rows // 2, features), dtype),
        in_specs=[IN_SMEM] + [IN_VMEM] * (1 + len(weights)),
        out_specs=IN_VMEM,
        scratch_shapes=[pltpu.VMEM((rows // 2, heads * HEAD_DIM), BF16)],
        compiler_params=pltpu.CompilerParams(vmem_limit_bytes=14 * 2**20),
        name="project",
    )(order, attended, *weights)


def norm_body(hidden, mine, other, gain, residual, normed):
    total = hidden[...].astype(F32) + mine[...] + other[...].astype(F32)
    residual[...] = total
    factor = lax.rsqrt(jnp.mean(total * total, axis=-1, keepdims=True) + EPSILON)
    normed[...] = (total * factor * gain[...]).astype(BF16)


def norm(hidden, mine, other, gain):
    return pl.pallas_call(
        norm_body,
        out_shape=(everywhere(hidden.shape, F32), everywhere(hidden.shape, BF16)),
        in_specs=[IN_VMEM] * 4,
        out_specs=(IN_VMEM,) * 2,
        compiler_params=pltpu.CompilerParams(vmem_limit_bytes=8 * 2**20),
        name="norm",
    )(hidden, mine, other, gain)


def stage_body(gate_up, down, *refs):
    count = gate_up.shape[0]
    sems = refs[2 * count]
    copies = []
    for expert in range(count):
        copies.append(pltpu.make_async_copy(gate_up.at[expert], refs[expert], sems.at[expert]))
        copies.append(pltpu.make_async_copy(down.at[expert], refs[count + expert], sems.at[count + expert]))
    for copy in copies:
        copy.start()
    for copy in copies:
        copy.wait()


def stage(gate_up, down):
    count = gate_up.shape[0]
    staged = pl.pallas_call(
        stage_body,
        out_shape=[pltpu.VMEM(gate_up.shape[1:], BF16)] * count + [pltpu.VMEM(down.shape[1:], BF16)] * count,
        in_specs=[IN_PLACE] * 2,
        out_specs=[IN_PLACE] * (2 * count),
        scratch_shapes=[pltpu.SemaphoreType.DMA((2 * count,))],
        compiler_params=pltpu.CompilerParams(vmem_limit_bytes=2**20),
        cost_estimate=pl.CostEstimate(flops=0, bytes_accessed=2 * (gate_up.size + down.size), transcendentals=0),
        name="stage",
    )(in_hbm(gate_up), in_hbm(down))
    return staged[:count], staged[count:]


def experts_body(per_pair, local_experts, first_expert, ids, gates, *refs):
    pairs, top, tokens = ids.shape
    gate_up, down, refs = refs[:local_experts], refs[local_experts : 2 * local_experts], refs[2 * local_experts :]
    sources = refs[: pairs * per_pair]
    same_core, other_core, picked, produced, hidden, chosen, slot_gates = refs[pairs * per_pair :]
    features, units = gate_up[0].shape[0], down[0].shape[0]
    slots = 2 * CAP
    earlier = lax.broadcasted_iota(jnp.int32, (tokens, tokens), 0)
    later = lax.broadcasted_iota(jnp.int32, (tokens, tokens), 1)
    before = jnp.where(earlier < later, 1.0, 0.0).astype(BF16)
    slot_ids = lax.broadcasted_iota(jnp.int32, (slots, tokens), 0).astype(F32)
    for pair in range(pairs):
        hits, shares = [], []
        for expert in range(local_experts):
            match = ids[pair] == (first_expert[0] + expert).astype(F32)
            hits.append(jnp.max(jnp.where(match, 1.0, 0.0), axis=0, keepdims=True))
            shares.append(jnp.sum(jnp.where(match, gates[pair], 0.0), axis=0, keepdims=True))
        stacked = jnp.concatenate(hits + [jnp.zeros((16 - local_experts, tokens), F32)], axis=0)
        places = jnp.dot(stacked.astype(BF16), before, preferred_element_type=F32)
        for expert in range(local_experts):
            place = jnp.where(hits[expert] > 0.5, places[expert : expert + 1], -1.0)
            taken = jnp.where(slot_ids == place, 1.0, 0.0)
            chosen[pair, expert * slots : (expert + 1) * slots, :] = taken.astype(BF16)
            slot_gates[expert, pair * slots : (pair + 1) * slots, :] = jnp.sum(
                taken * shares[expert], axis=1, keepdims=True
            )
        group = sources[pair * per_pair : (pair + 1) * per_pair]
        step = 512
        for column in range(0, features, step):
            rows = jnp.concatenate([ref[:, column : column + step] for ref in group], axis=0)
            found = jnp.dot(chosen[pair], rows, preferred_element_type=F32).astype(BF16)
            for expert in range(local_experts):
                picked[expert, pair * slots : (pair + 1) * slots, column : column + step] = found[
                    expert * slots : (expert + 1) * slots
                ]
    chunk = slots * min(pairs, 4)
    for expert in range(local_experts):
        for low in range(0, pairs * slots, chunk):
            rows = picked[expert, low : low + chunk, :]
            gate_rows = slot_gates[expert, low : low + chunk, :]
            for column in range(0, units, 256):
                gate = jnp.dot(rows, gate_up[expert][:, column : column + 256], preferred_element_type=F32)
                up = jnp.dot(
                    rows, gate_up[expert][:, units + column : units + column + 256], preferred_element_type=F32
                )
                active = gate / (1.0 + jnp.exp(-gate)) * up * gate_rows
                hidden[low : low + chunk, column : column + 256] = active.astype(BF16)
            for column in range(0, features, 512):
                result = jnp.dot(
                    hidden[low : low + chunk, :], down[expert][:, column : column + 512], preferred_element_type=F32
                ).astype(BF16)
                for inner in range(chunk // slots):
                    produced[
                        low // slots + inner, expert * slots : (expert + 1) * slots, column : column + 512
                    ] = result[inner * slots : (inner + 1) * slots]
    for pair in range(pairs):
        for column in range(0, features, 512):
            mixture = lax.dot_general(
                chosen[pair], produced[pair, :, column : column + 512], (((0,), (0,)), ((), ())),
                preferred_element_type=F32,
            ).astype(BF16)
            same_core[pair, :, column : column + 512] = mixture[: tokens // 2]
            other_core[pair, :, column : column + 512] = mixture[tokens // 2 :]


def experts(first_expert, ids, gates, gate_up, down, sources, limit, pin=False):
    pairs, top, tokens = ids.shape
    local_experts, (features, _) = len(gate_up), gate_up[0].shape
    units = down[0].shape[0]
    slots = 2 * CAP
    matrices = [*gate_up, *down]
    if pin:
        matrices = [in_vmem(part) for part in matrices]
    return pl.pallas_call(
        lambda *refs: experts_body(len(sources) // pairs, local_experts, *refs),
        out_shape=(everywhere((pairs, tokens // 2, features), BF16),) * 2,
        in_specs=[IN_SMEM] + [IN_VMEM] * (2 + 2 * local_experts + len(sources)),
        out_specs=(IN_VMEM,) * 2,
        scratch_shapes=[
            pltpu.VMEM((local_experts, pairs * slots, features), BF16),
            pltpu.VMEM((pairs, local_experts * slots, features), BF16),
            pltpu.VMEM((pairs * slots, units), BF16),
            pltpu.VMEM((pairs, local_experts * slots, tokens), BF16),
            pltpu.VMEM((local_experts, pairs * slots, 1), F32),
        ],
        compiler_params=pltpu.CompilerParams(vmem_limit_bytes=limit),
        cost_estimate=pl.CostEstimate(
            flops=12 * local_experts * pairs * slots * features * units, bytes_accessed=16 * 2**20, transcendentals=0
        ),
        name="experts",
    )(first_expert, ids, gates, *matrices, *sources)


def add_rows(left, right):
    return (left.astype(F32) + right.astype(F32)).astype(BF16)


def on_planes(
    hidden_in, tree_queries, tree_keys, tree_values, parents, accepted, tree_parents, request_prompt, prompt_lengths,
    prompt_keys, prompt_values, out_proj, gain, expert_ids, gate_weights, gate_up, down,
):
    tok_rows, features = hidden_in.shape
    prompt_count, rows_here, _ = prompt_keys.shape
    me = lax.axis_index("ep").astype(jnp.int32)

    flat = (prompt_count * rows_here, features)
    send, send_prompts, prompts, block = pack(
        me.reshape(1), tree_queries, tree_keys, tree_values, prompt_keys.reshape(flat),
        prompt_values.reshape(flat), expert_ids.T, gate_weights.T, out_proj,
    )
    x_mine, y_mine = flip(prompts, 2, 8), flip(prompts, 4, 8)
    theirs = flip(send_prompts, 1, 8)
    x_theirs, y_theirs = flip(theirs, 2, 8), flip(theirs, 4, 8)
    far_a, far_b = flip(x_mine, 4, 8), flip(y_theirs, 2, 8)
    weights, pieces, order, up, down_rows = fetch_projection(out_proj, block, (x_mine, y_mine, x_theirs, y_theirs, far_a, far_b))
    got = flip(send, 1, 8)
    small = jnp.concatenate(
        [tree_parents, jnp.broadcast_to(request_prompt[:, None], tree_parents.shape)], axis=0
    )
    sibling = flip(after(small, x_mine), 1, 8)

    column = jnp.arange(8 * flat[0], dtype=jnp.int32)
    columns = jnp.stack([column // flat[0], column % flat[0] // rows_here, column % rows_here])
    chip_parents = jnp.concatenate([tree_parents, sibling[: tree_parents.shape[0]]], axis=0)
    first_node = jnp.arange(chip_parents.shape[0], dtype=jnp.int32)[:, None] * tree_parents.shape[1]
    chip_parents = jnp.where(chip_parents < 0, -1, chip_parents + first_node).reshape(-1, 1)
    attended, cache, ids, gates = chip_attention(
        (me.reshape(1), request_prompt, sibling, prompt_lengths), columns, chip_parents, accepted,
        tree_queries, tree_keys, tree_values, prompts, (got, theirs, x_mine, x_theirs, y_mine, y_theirs, far_a, far_b),
    )
    up, down_rows = after((up, down_rows), attended)
    edge = up.shape[0] // 2
    last_first, last_second = [
        jnp.where(lax.axis_index("rep") >= 2, up[rows], down_rows[rows]) for rows in (slice(0, edge), slice(edge, None))
    ]
    weights += [last_first, last_second, flip(last_first, 2, 8), flip(last_second, 4, 8)]
    other = flip(chip_project(order, attended, weights, pieces, tok_rows, BF16), 1, 8)
    mine = chip_project(order, attended, weights, pieces, 0, F32)
    residual, normed = norm(hidden_in, mine, other, gain)

    across, from_x, from_y = flip(normed, 6, 8), flip(normed, 2, 8), flip(normed, 4, 8)
    sibling_rows = flip(normed, 1, 8)
    first_expert = (me * gate_up.shape[0]).reshape(1)
    gate_up, down = stage(*after((gate_up, down), normed))

    def run(low, high, sources, megabytes, *done):
        return experts(
            first_expert, after(ids[low:high], done), gates[low:high], gate_up, down, sources, megabytes * 2**20, True
        )

    near_same, near_other = run(0, 1, [normed, sibling_rows], 12)
    across = after(across, near_same)
    far_same, far_other = run(3, 4, [across, flip(across, 1, 8)], 12)
    far = add_rows(far_same, flip(far_other, 1, 8))[0]

    half = tok_rows // 2
    far_first, far_second = flip(far[:half], 2, 8), flip(far[half:], 4, 8)
    beside = [from_x, flip(from_x, 1, 8), from_y, flip(from_y, 1, 8)]
    side_same, side_other = run(1, 3, beside, 16, far)
    side = [part.astype(F32) for part in (side_same, flip(after(side_other, far_first, far_second), 1, 8))]
    side = side[0] + side[1]
    to_x = jnp.concatenate([side[0, :half], side[0, half:] + far_second.astype(F32)], axis=0).astype(BF16)
    to_y = jnp.concatenate([side[1, :half] + far_first.astype(F32), side[1, half:]], axis=0).astype(BF16)
    terms = [near_same[0], flip(near_other, 1, 8)[0], flip(to_x, 2, 8), flip(to_y, 4, 8)]
    return residual, terms, cache


def on_any_mesh(
    hidden_in, tree_queries, tree_keys, tree_values, parents, accepted, tree_parents, request_prompt, prompt_lengths,
    prompt_keys, prompt_values, out_proj, gain, expert_ids, gate_weights, gate_up, down,
):
    tok_rows, features = hidden_in.shape
    prompt_count, rows_here, _ = prompt_keys.shape
    ep_size = lax.axis_size("ep")
    me = lax.axis_index("ep").astype(jnp.int32)
    keys = lax.all_gather(prompt_keys, "ep", axis=1, tiled=True).reshape(-1, features)
    values = lax.all_gather(prompt_values, "ep", axis=1, tiled=True).reshape(-1, features)
    column = jnp.arange(keys.shape[0], dtype=jnp.int32)
    columns = jnp.stack([column // (rows_here * ep_size), column % (rows_here * ep_size)])
    attended, cache = plain_attention(
        request_prompt, prompt_lengths, columns, parents, accepted, tree_queries, tree_keys, tree_values, keys, values
    )
    joined = lax.all_gather(out_proj, "rep", axis=0, tiled=True)
    projected = jnp.dot(attended, joined, preferred_element_type=F32)
    residual, normed = norm(hidden_in, projected, jnp.zeros(hidden_in.shape, BF16), gain)
    routing = jnp.concatenate([expert_ids.astype(F32).T, gate_weights.T], axis=0)
    routing = lax.all_gather(routing, "ep", axis=0).reshape(ep_size // 2, 2, -1, tok_rows)
    routing = jnp.concatenate([routing[:, 0], routing[:, 1]], axis=-1)
    top = expert_ids.shape[1]
    everyone = lax.all_gather(normed, "ep", axis=0, tiled=True)
    sources = [everyone[i * 2 * tok_rows : (i + 1) * 2 * tok_rows] for i in range(ep_size // 2)]
    same_core, other_core = experts(
        (me * gate_up.shape[0]).reshape(1), routing[:, :top], routing[:, top:], list(gate_up), list(down), sources,
        VMEM_LIMIT
    )
    shares = jnp.stack([same_core, other_core], axis=1).reshape(ep_size, tok_rows, features)
    shares = lax.all_to_all(shares, "ep", split_axis=0, concat_axis=0, tiled=True)
    return residual, [shares[i] for i in range(ep_size)], cache


def per_device(
    hidden_in,
    tree_queries,
    tree_keys,
    tree_values,
    tree_parents,
    accepted_nodes,
    request_prompt,
    prompt_lengths,
    prompt_keys,
    prompt_values,
    out_proj,
    norm_gain,
    expert_ids,
    gate_weights,
    expert_gate_up,
    expert_down,
):
    tok_rows, features = hidden_in.shape
    req_count, tree_len = tree_parents.shape
    first_node = jnp.arange(req_count, dtype=jnp.int32)[:, None] * tree_len
    accepted = (first_node + accepted_nodes).reshape(-1, 1)
    parents = jnp.where(tree_parents < 0, -1, tree_parents + first_node).reshape(-1, 1)
    planes = lax.axis_size("ep") == 8 and lax.axis_size("rep") == 4 and out_proj.shape[0] == 4 * HEAD_DIM
    plan = on_planes if planes else on_any_mesh
    residual, terms, cache = plan(
        hidden_in, tree_queries, tree_keys, tree_values, parents, accepted, tree_parents, request_prompt,
        prompt_lengths, prompt_keys, prompt_values, out_proj, norm_gain.reshape(1, features), expert_ids,
        gate_weights, expert_gate_up, expert_down,
    )
    layer_out = residual
    for term in terms:
        layer_out = layer_out + term.astype(F32)
    accepted_cache = cache.reshape(req_count, accepted_nodes.shape[1], 2 * features)
    return (layer_out.astype(BF16), accepted_cache)


def solution(mesh):
    in_specs = (
        P(("rep", "ep"), None),
        P(("rep", "ep"), None),
        P(("rep", "ep"), None),
        P(("rep", "ep"), None),
        P(("rep", "ep"), None),
        P(("rep", "ep"), None),
        P(("rep", "ep")),
        P("rep"),
        P("rep", "ep", None),
        P("rep", "ep", None),
        P("rep", None),
        P(),
        P(("rep", "ep"), None),
        P(("rep", "ep"), None),
        P("ep", None, None),
        P("ep", None, None),
    )
    out_specs = (P(("rep", "ep"), None), P(("rep", "ep"), None, None))
    return jax.shard_map(
        per_device, mesh=mesh, in_specs=in_specs, out_specs=out_specs, check_vma=False
    )
```

```python
import math

import jax
import jax.numpy as jnp
from jax import lax
from jax.experimental import pallas as pl
from jax.experimental.pallas import tpu as pltpu
from jax.sharding import PartitionSpec as P

HEADS = 16
HEAD_DIM = 128
CAP = 40

NEG_FILL = -1e30
EPSILON = 1e-05
VMEM_LIMIT = 56 * 1024 * 1024

F32 = jnp.float32
BF16 = jnp.bfloat16


def flip(value, bits, size):
    return lax.ppermute(value, "ep", [(i, i ^ bits) for i in range(size)])


def in_hbm(value):
    return pltpu.with_memory_space_constraint(value, pltpu.HBM)


def in_vmem(value):
    return pltpu.with_memory_space_constraint(value, pltpu.VMEM)


def after(value, *done):
    return lax.optimization_barrier((value, done))[0]


def everywhere(shape, dtype):
    return jax.ShapeDtypeStruct(shape, dtype)


IN_VMEM = pl.BlockSpec(memory_space=pltpu.VMEM)
IN_SMEM = pl.BlockSpec(memory_space=pltpu.SMEM)
IN_PLACE = pl.BlockSpec(memory_space=pl.ANY)


def pack_body(place, *refs):
    sources, out_proj, (send, send_prompts, prompts, block) = refs[:7], refs[7], refs[8:12]
    held, sems = refs[12:19], refs[19]
    core, parity = place[0] % 2, (place[0] // 2 + place[0] // 4) % 2
    head_rows = pl.ds(pl.multiple_of((2 * core + parity) * HEAD_DIM, HEAD_DIM), HEAD_DIM)
    copies = [pltpu.make_async_copy(sources[i], held[i], sems.at[i]) for i in range(7)]
    copies.append(pltpu.make_async_copy(out_proj.at[head_rows], block, sems.at[7]))
    for copy in copies:
        copy.start()
    for copy in copies:
        copy.wait()
    queries, keys, values, prompt_keys, prompt_values, ids, gates = held
    rows, features = queries.shape
    shards = features // (4 * HEAD_DIM)
    width = 2 * HEAD_DIM
    for shard in range(shards):
        lanes = slice(shard * width, (shard + 1) * width)
        for target, which in ((0, core), (1, 1 - core)):
            start = pl.multiple_of(shard * 2 * width + which * width, width)
            low = 0
            for part in (queries, keys, values, prompt_keys, prompt_values):
                high = low + part.shape[0]
                if high > 3 * rows:
                    kept = slice(low - 3 * rows, high - 3 * rows)
                    (prompts, send_prompts)[target][kept, lanes] = part[:, pl.ds(start, width)]
                elif target == 1:
                    send[low:high, lanes] = part[:, pl.ds(start, width)]
                low = high
    top = ids.shape[0]
    high_part = gates[...].astype(BF16)
    low_part = (gates[...] - high_part.astype(F32)).astype(BF16)
    blank = jnp.zeros((top, rows), F32)
    first = jnp.concatenate([ids[...].astype(F32), high_part.astype(F32)], axis=0).astype(BF16)
    second = jnp.concatenate([blank, low_part.astype(F32)], axis=0).astype(BF16)
    base = 2 * prompt_keys.shape[0]
    for target in (send_prompts, prompts):
        target[base : base + 2 * top, :] = jnp.zeros((2 * top, target.shape[1]), BF16)
        target[base : base + 2 * top, :rows] = first
        target[base : base + 2 * top, rows : 2 * rows] = second


def pack(place, queries, keys, values, prompt_keys, prompt_values, ids, gates, out_proj):
    rows, features = queries.shape
    tail = 2 * prompt_keys.shape[0] + 2 * ids.shape[0]
    parts = (queries, keys, values, prompt_keys, prompt_values, ids, gates)
    return pl.pallas_call(
        pack_body,
        out_shape=(
            everywhere((3 * rows, features // 2), BF16),
            everywhere((tail, features // 2), BF16),
            everywhere((tail, features // 2), BF16),
            everywhere((HEAD_DIM, features), BF16),
        ),
        in_specs=[IN_SMEM] + [IN_PLACE] * 8,
        out_specs=(IN_VMEM,) * 4,
        scratch_shapes=[pltpu.VMEM(part.shape, part.dtype) for part in parts] + [pltpu.SemaphoreType.DMA((8,))],
        compiler_params=pltpu.CompilerParams(vmem_limit_bytes=12 * 2**20),
        name="pack",
    )(place, *[in_hbm(part) for part in (*parts, out_proj)])


def attend(queries, all_keys, all_values, bias):
    scores = lax.dot_general(queries, all_keys, (((1,), (1,)), ((), ())), preferred_element_type=F32)
    scores = scores * (1.0 / math.sqrt(HEAD_DIM)) + bias
    weights = jnp.exp(scores - jnp.max(scores, axis=-1, keepdims=True))
    total = jnp.sum(weights, axis=-1, keepdims=True)
    mixed = jnp.dot(weights.astype(BF16), all_values, preferred_element_type=F32)
    return (mixed / total).astype(BF16)


def fill_bias(bias, prompt_rows, tree_len, parents, prompts, lengths, prompt_of, position):
    tokens = bias.shape[0]
    for request in range(tokens // tree_len):
        prompt = prompts[request]
        seen = (prompt_of == prompt) & (position < lengths[prompt])
        row = jnp.where(seen, 0.0, NEG_FILL)
        bias[request * tree_len : (request + 1) * tree_len, :prompt_rows] = jnp.broadcast_to(
            row, (tree_len, prompt_rows)
        )
    node = lax.broadcasted_iota(jnp.int32, (tokens, tokens), 0)
    other = lax.broadcasted_iota(jnp.int32, (tokens, tokens), 1)
    reach = jnp.where((other == parents) | (other == node), 1.0, 0.0)
    for _ in range((tree_len - 1).bit_length()):
        reach = reach.astype(BF16)
        reach = jnp.minimum(jnp.dot(reach, reach, preferred_element_type=F32), 1.0)
    bias[:, prompt_rows:] = jnp.where(reach > 0.5, 0.0, NEG_FILL)


def accepted_body(accepted, tree_keys, tree_values, cache):
    rows, features = tree_keys.shape
    chosen = accepted[...] == lax.broadcasted_iota(jnp.int32, (accepted.shape[0], rows), 1)
    chosen = jnp.where(chosen, 1.0, 0.0).astype(BF16)
    cache[:, :features] = jnp.dot(chosen, tree_keys[...], preferred_element_type=F32).astype(BF16)
    cache[:, features:] = jnp.dot(chosen, tree_values[...], preferred_element_type=F32).astype(BF16)


def chip_attention_body(
    me, my_prompts, sibling, lengths, columns, parents, accepted, prompts_here, got, *refs
):
    copies = [pltpu.make_async_copy(refs[i], refs[15 + i], refs[25].at[i]) for i in range(10)]
    for copy in copies:
        copy.start()
    (attended, cache, ids, gates, bias), (queries_here, tree_keys, tree_values, *holders) = refs[10:15], refs[15:25]
    holders = [prompts_here, *holders]
    rows = tree_keys.shape[0]
    requests = my_prompts.shape[0]
    tree_len = rows // requests
    block = (holders[0].shape[0] - 16) // 2
    prompts = [my_prompts[i] for i in range(requests)] + [sibling[requests + i, 0] for i in range(requests)]
    position = (columns[0:1, :] ^ me[0]) * (block // lengths.shape[0]) + columns[2:3, :]
    fill_bias(bias, columns.shape[1], tree_len, parents[...], prompts, lengths, columns[1:2, :], position)
    for copy in copies:
        copy.wait()
    for head in range(got.shape[1] // HEAD_DIM):
        lanes = slice(head * HEAD_DIM, (head + 1) * HEAD_DIM)
        place = head // 2 * 4 * HEAD_DIM + me[0] % 2 * 2 * HEAD_DIM + head % 2 * HEAD_DIM
        mine = pl.ds(pl.multiple_of(place, HEAD_DIM), HEAD_DIM)
        queries = jnp.concatenate([queries_here[:, mine], got[:rows, lanes]], axis=0)
        all_keys = jnp.concatenate(
            [ref[:block, lanes] for ref in holders]
            + [tree_keys[:, mine], got[rows : 2 * rows, lanes]],
            axis=0,
        )
        all_values = jnp.concatenate(
            [ref[block : 2 * block, lanes] for ref in holders]
            + [tree_values[:, mine], got[2 * rows : 3 * rows, lanes]],
            axis=0,
        )
        attended[head] = attend(queries, all_keys, all_values, bias[...])
    accepted_body(accepted, tree_keys, tree_values, cache)
    for index, ref in enumerate(holders):
        first = ref[2 * block :, :rows].astype(F32)
        second = ref[2 * block :, rows : 2 * rows].astype(F32)
        lanes = slice(index % 2 * rows, (index % 2 + 1) * rows)
        ids[index // 2, :, lanes] = first[:8]
        gates[index // 2, :, lanes] = first[8:] + second[8:]


def chip_attention(scalars, columns, parents, accepted, queries, tree_keys, tree_values, prompts, got, blocks):
    rows, features = tree_keys.shape
    width = columns.shape[1] + 2 * rows
    heads = features // HEAD_DIM // 2
    copied = [in_hbm(part) for part in (queries, tree_keys, tree_values, *blocks)]
    return pl.pallas_call(
        chip_attention_body,
        out_shape=(
            everywhere((heads, 2 * rows, HEAD_DIM), BF16),
            everywhere((accepted.shape[0], 2 * features), BF16),
            everywhere((4, 8, 2 * rows), F32),
            everywhere((4, 8, 2 * rows), F32),
        ),
        in_specs=[IN_SMEM] * 4 + [IN_VMEM] * 5 + [IN_PLACE] * len(copied),
        out_specs=(IN_VMEM,) * 4,
        scratch_shapes=[pltpu.VMEM((2 * rows, width), F32)]
        + [pltpu.VMEM(part.shape, BF16) for part in copied]
        + [pltpu.SemaphoreType.DMA((len(copied),))],
        compiler_params=pltpu.CompilerParams(vmem_limit_bytes=14 * 2**20),
        name="attention",
    )(*scalars, columns, parents, accepted, prompts, got, *copied)


def plain_attention_body(
    prompts, lengths, columns, parents, accepted, queries, tree_keys, tree_values, keys, values, attended, cache, bias
):
    rows, features = queries.shape
    tree_len = rows // prompts.shape[0]
    requests = [prompts[i] for i in range(prompts.shape[0])]
    fill_bias(bias, columns.shape[1], tree_len, parents[...], requests, lengths, columns[0:1, :], columns[1:2, :])
    for head in range(features // HEAD_DIM):
        lanes = slice(head * HEAD_DIM, (head + 1) * HEAD_DIM)
        all_keys = jnp.concatenate([keys[:, lanes], tree_keys[:, lanes]], axis=0)
        all_values = jnp.concatenate([values[:, lanes], tree_values[:, lanes]], axis=0)
        attended[:, lanes] = attend(queries[:, lanes], all_keys, all_values, bias[...])
    accepted_body(accepted, tree_keys, tree_values, cache)


def plain_attention(prompts, lengths, columns, parents, accepted, queries, tree_keys, tree_values, keys, values):
    rows, features = queries.shape
    return pl.pallas_call(
        plain_attention_body,
        out_shape=(everywhere((rows, features), BF16), everywhere((accepted.shape[0], 2 * features), BF16)),
        in_specs=[IN_SMEM] * 2 + [IN_VMEM] * 8,
        out_specs=(IN_VMEM,) * 2,
        scratch_shapes=[pltpu.VMEM((rows, columns.shape[1] + rows), F32)],
        compiler_params=pltpu.CompilerParams(vmem_limit_bytes=VMEM_LIMIT),
        name="attention",
    )(prompts, lengths, columns, parents, accepted, queries, tree_keys, tree_values, keys, values)


def fetch_projection(out_proj, block, before_shared):
    me, place = lax.axis_index("rep"), lax.axis_index("ep")
    core, parity = place % 2, (place // 2 + place // 4) % 2
    own = lax.dynamic_slice_in_dim(out_proj, core * 2 * HEAD_DIM, 2 * HEAD_DIM, 0)

    def shifted(value, by):
        return lax.ppermute(value, "rep", [(i, (i + by) % 4) for i in range(4)])

    came1, came3 = shifted(block, 1), shifted(block, 3)
    up = lax.ppermute(came1, "rep", [(1, 2), (2, 3)])
    down = lax.ppermute(came3, "rep", [(2, 1), (1, 0)])
    order = [2 * me, 2 * me + 1]
    for by in (1, 3, 2):
        shard = (me + 4 - by) % 4
        order += [2 * shard + parity, 2 * shard + 1 - parity]
    half = HEAD_DIM // 2
    came1, came3 = after((came1, came3), before_shared)
    first = jnp.concatenate([came1[:half], came3[:half]], axis=0)
    second = jnp.concatenate([came1[half:], came3[half:]], axis=0)
    from_x, from_y = flip(first, 2, 8), flip(second, 4, 8)
    weights = [own, first, second, from_x, from_y]
    pieces = [(0, 0, 2 * HEAD_DIM)]
    for low in (0, half):
        pieces += [(index, low, low + half) for index in (1, 2, 3, 4)]
    pieces += [(index, 0, half) for index in (5, 6, 7, 8)]
    return weights, pieces, jnp.stack(order).astype(jnp.int32), up, down


def chip_project_body(pieces, low_row, order, attended, *refs):
    weights, (result, ordered) = refs[: len(refs) - 2], refs[len(refs) - 2 :]
    rows, features = result.shape
    for index in range(attended.shape[0]):
        ordered[:, index * HEAD_DIM : (index + 1) * HEAD_DIM] = attended[order[index], low_row : low_row + rows, :]
    step = 256
    for column in range(0, features, step):
        joined = jnp.concatenate(
            [weights[ref][low:high, column : column + step] for ref, low, high in pieces], axis=0
        )
        total = jnp.dot(ordered[...], joined, preferred_element_type=F32)
        result[:, column : column + step] = total.astype(result.dtype)


def chip_project(order, attended, weights, pieces, low_row, dtype):
    heads, rows, _ = attended.shape
    features = weights[0].shape[1]
    return pl.pallas_call(
        lambda *refs: chip_project_body(pieces, low_row, *refs),
        out_shape=everywhere((rows // 2, features), dtype),
        in_specs=[IN_SMEM] + [IN_VMEM] * (1 + len(weights)),
        out_specs=IN_VMEM,
        scratch_shapes=[pltpu.VMEM((rows // 2, heads * HEAD_DIM), BF16)],
        compiler_params=pltpu.CompilerParams(vmem_limit_bytes=14 * 2**20),
        name="project",
    )(order, attended, *weights)


def norm_body(hidden, mine, other, gain, residual, normed):
    total = hidden[...].astype(F32) + mine[...] + other[...].astype(F32)
    residual[...] = total
    factor = lax.rsqrt(jnp.mean(total * total, axis=-1, keepdims=True) + EPSILON)
    normed[...] = (total * factor * gain[...]).astype(BF16)


def norm(hidden, mine, other, gain):
    return pl.pallas_call(
        norm_body,
        out_shape=(everywhere(hidden.shape, F32), everywhere(hidden.shape, BF16)),
        in_specs=[IN_VMEM] * 4,
        out_specs=(IN_VMEM,) * 2,
        compiler_params=pltpu.CompilerParams(vmem_limit_bytes=8 * 2**20),
        name="norm",
    )(hidden, mine, other, gain)


def stage_body(gate_up, down, *refs):
    count = gate_up.shape[0]
    sems = refs[2 * count]
    copies = []
    for expert in range(count):
        copies.append(pltpu.make_async_copy(gate_up.at[expert], refs[expert], sems.at[expert]))
        copies.append(pltpu.make_async_copy(down.at[expert], refs[count + expert], sems.at[count + expert]))
    for copy in copies:
        copy.start()
    for copy in copies:
        copy.wait()


def stage(gate_up, down):
    count = gate_up.shape[0]
    staged = pl.pallas_call(
        stage_body,
        out_shape=[pltpu.VMEM(gate_up.shape[1:], BF16)] * count + [pltpu.VMEM(down.shape[1:], BF16)] * count,
        in_specs=[IN_PLACE] * 2,
        out_specs=[IN_PLACE] * (2 * count),
        scratch_shapes=[pltpu.SemaphoreType.DMA((2 * count,))],
        compiler_params=pltpu.CompilerParams(vmem_limit_bytes=2**20),
        cost_estimate=pl.CostEstimate(flops=0, bytes_accessed=2 * (gate_up.size + down.size), transcendentals=0),
        name="stage",
    )(in_hbm(gate_up), in_hbm(down))
    return staged[:count], staged[count:]


def route_body(local_experts, first_expert, ids, gates, chosen, slot_gates):
    pairs, top, tokens = ids.shape
    slots = 2 * CAP
    earlier = lax.broadcasted_iota(jnp.int32, (tokens, tokens), 0)
    later = lax.broadcasted_iota(jnp.int32, (tokens, tokens), 1)
    before = jnp.where(earlier < later, 1.0, 0.0).astype(BF16)
    slot_ids = lax.broadcasted_iota(jnp.int32, (slots, tokens), 0).astype(F32)
    for pair in range(pairs):
        hits, shares = [], []
        for expert in range(local_experts):
            match = ids[pair] == (first_expert[0] + expert).astype(F32)
            hits.append(jnp.max(jnp.where(match, 1.0, 0.0), axis=0, keepdims=True))
            shares.append(jnp.sum(jnp.where(match, gates[pair], 0.0), axis=0, keepdims=True))
        stacked = jnp.concatenate(hits + [jnp.zeros((16 - local_experts, tokens), F32)], axis=0)
        places = jnp.dot(stacked.astype(BF16), before, preferred_element_type=F32)
        for expert in range(local_experts):
            place = jnp.where(hits[expert] > 0.5, places[expert : expert + 1], -1.0)
            taken = jnp.where(slot_ids == place, 1.0, 0.0)
            rows = slice(expert * slots, (expert + 1) * slots)
            chosen[pair, rows, :] = taken.astype(BF16)
            slot_gates[pair, rows, :] = jnp.sum(taken * shares[expert], axis=1, keepdims=True)


def route(first_expert, ids, gates, local_experts):
    pairs, top, tokens = ids.shape
    rows = local_experts * 2 * CAP
    return pl.pallas_call(
        lambda *refs: route_body(local_experts, *refs),
        out_shape=(everywhere((pairs, rows, tokens), BF16), everywhere((pairs, rows, 1), F32)),
        in_specs=[IN_SMEM, IN_VMEM, IN_VMEM],
        out_specs=(IN_VMEM,) * 2,
        compiler_params=pltpu.CompilerParams(vmem_limit_bytes=24 * 2**20),
        name="route",
    )(first_expert, ids, gates)


def experts_body(per_pair, local_experts, chosen, slot_gates, *refs):
    pairs, _, tokens = chosen.shape
    gate_up, down, refs = refs[:local_experts], refs[local_experts : 2 * local_experts], refs[2 * local_experts :]
    sources = refs[: pairs * per_pair]
    same_core, other_core, picked, produced, hidden = refs[pairs * per_pair :]
    features, units = gate_up[0].shape[0], down[0].shape[0]
    slots = 2 * CAP
    for pair in range(pairs):
        group = sources[pair * per_pair : (pair + 1) * per_pair]
        step = 512
        for column in range(0, features, step):
            rows = jnp.concatenate([ref[:, column : column + step] for ref in group], axis=0)
            found = jnp.dot(chosen[pair], rows, preferred_element_type=F32).astype(BF16)
            for expert in range(local_experts):
                picked[expert, pair * slots : (pair + 1) * slots, column : column + step] = found[
                    expert * slots : (expert + 1) * slots
                ]
    chunk = slots * min(pairs, 4)
    for expert in range(local_experts):
        for low in range(0, pairs * slots, chunk):
            rows = picked[expert, low : low + chunk, :]
            gate_rows = jnp.concatenate(
                [
                    slot_gates[low // slots + inner, expert * slots : (expert + 1) * slots, :]
                    for inner in range(chunk // slots)
                ],
                axis=0,
            )
            for column in range(0, units, 256):
                gate = jnp.dot(rows, gate_up[expert][:, column : column + 256], preferred_element_type=F32)
                up = jnp.dot(
                    rows, gate_up[expert][:, units + column : units + column + 256], preferred_element_type=F32
                )
                active = gate / (1.0 + jnp.exp(-gate)) * up * gate_rows
                hidden[low : low + chunk, column : column + 256] = active.astype(BF16)
            for column in range(0, features, 512):
                result = jnp.dot(
                    hidden[low : low + chunk, :], down[expert][:, column : column + 512], preferred_element_type=F32
                ).astype(BF16)
                for inner in range(chunk // slots):
                    produced[
                        low // slots + inner, expert * slots : (expert + 1) * slots, column : column + 512
                    ] = result[inner * slots : (inner + 1) * slots]
    for pair in range(pairs):
        for column in range(0, features, 512):
            mixture = lax.dot_general(
                chosen[pair], produced[pair, :, column : column + 512], (((0,), (0,)), ((), ())),
                preferred_element_type=F32,
            ).astype(BF16)
            same_core[pair, :, column : column + 512] = mixture[: tokens // 2]
            other_core[pair, :, column : column + 512] = mixture[tokens // 2 :]


def experts(chosen, slot_gates, gate_up, down, sources, limit, pin=False):
    pairs, _, tokens = chosen.shape
    local_experts, (features, _) = len(gate_up), gate_up[0].shape
    units = down[0].shape[0]
    slots = 2 * CAP
    matrices = [*gate_up, *down]
    if pin:
        matrices = [in_vmem(part) for part in matrices]
    return pl.pallas_call(
        lambda *refs: experts_body(len(sources) // pairs, local_experts, *refs),
        out_shape=(everywhere((pairs, tokens // 2, features), BF16),) * 2,
        in_specs=[IN_VMEM] * (2 + 2 * local_experts + len(sources)),
        out_specs=(IN_VMEM,) * 2,
        scratch_shapes=[
            pltpu.VMEM((local_experts, pairs * slots, features), BF16),
            pltpu.VMEM((pairs, local_experts * slots, features), BF16),
            pltpu.VMEM((pairs * slots, units), BF16),
        ],
        compiler_params=pltpu.CompilerParams(vmem_limit_bytes=limit),
        cost_estimate=pl.CostEstimate(
            flops=12 * local_experts * pairs * slots * features * units, bytes_accessed=16 * 2**20, transcendentals=0
        ),
        name="experts",
    )(chosen, slot_gates, *matrices, *sources)


def add_rows(left, right):
    return (left.astype(F32) + right.astype(F32)).astype(BF16)


def on_planes(
    hidden_in, tree_queries, tree_keys, tree_values, parents, accepted, tree_parents, request_prompt, prompt_lengths,
    prompt_keys, prompt_values, out_proj, gain, expert_ids, gate_weights, gate_up, down,
):
    tok_rows, features = hidden_in.shape
    prompt_count, rows_here, _ = prompt_keys.shape
    me = lax.axis_index("ep").astype(jnp.int32)

    flat = (prompt_count * rows_here, features)
    send, send_prompts, prompts, block = pack(
        me.reshape(1), tree_queries, tree_keys, tree_values, prompt_keys.reshape(flat),
        prompt_values.reshape(flat), expert_ids.T, gate_weights.T, out_proj,
    )
    x_mine, y_mine = flip(prompts, 2, 8), flip(prompts, 4, 8)
    theirs = flip(send_prompts, 1, 8)
    x_theirs, y_theirs = flip(theirs, 2, 8), flip(theirs, 4, 8)
    far_a, far_b = flip(x_mine, 4, 8), flip(y_theirs, 2, 8)
    weights, pieces, order, up, down_rows = fetch_projection(out_proj, block, (x_mine, y_mine, x_theirs, y_theirs, far_a, far_b))
    got = flip(send, 1, 8)
    small = jnp.concatenate(
        [tree_parents, jnp.broadcast_to(request_prompt[:, None], tree_parents.shape)], axis=0
    )
    sibling = flip(after(small, x_mine), 1, 8)

    column = jnp.arange(8 * flat[0], dtype=jnp.int32)
    columns = jnp.stack([column // flat[0], column % flat[0] // rows_here, column % rows_here])
    chip_parents = jnp.concatenate([tree_parents, sibling[: tree_parents.shape[0]]], axis=0)
    first_node = jnp.arange(chip_parents.shape[0], dtype=jnp.int32)[:, None] * tree_parents.shape[1]
    chip_parents = jnp.where(chip_parents < 0, -1, chip_parents + first_node).reshape(-1, 1)
    attended, cache, ids, gates = chip_attention(
        (me.reshape(1), request_prompt, sibling, prompt_lengths), columns, chip_parents, accepted,
        tree_queries, tree_keys, tree_values, prompts, got, (theirs, x_mine, x_theirs, y_mine, y_theirs, far_a, far_b),
    )
    up, down_rows = after((up, down_rows), attended)
    edge = up.shape[0] // 2
    last_first, last_second = [
        jnp.where(lax.axis_index("rep") >= 2, up[rows], down_rows[rows]) for rows in (slice(0, edge), slice(edge, None))
    ]
    weights += [last_first, last_second, flip(last_first, 2, 8), flip(last_second, 4, 8)]
    chosen, slot_gates = route((me * gate_up.shape[0]).reshape(1), after(ids, last_first), gates, gate_up.shape[0])
    attended = after(attended, chosen)
    other = flip(chip_project(order, attended, weights, pieces, tok_rows, BF16), 1, 8)
    mine = chip_project(order, attended, weights, pieces, 0, F32)
    residual, normed = norm(hidden_in, mine, other, gain)

    across, from_x, from_y = flip(normed, 6, 8), flip(normed, 2, 8), flip(normed, 4, 8)
    sibling_rows = flip(normed, 1, 8)
    gate_up, down = stage(*after((gate_up, down), normed))

    def run(low, high, sources, megabytes, *done):
        return experts(
            after(chosen[low:high], done), slot_gates[low:high], gate_up, down, sources, megabytes * 2**20, True
        )

    near_same, near_other = run(0, 1, [normed, sibling_rows], 12)
    across = after(across, near_same)
    far_same, far_other = run(3, 4, [across, flip(across, 1, 8)], 12)
    far = add_rows(far_same, flip(far_other, 1, 8))[0]

    half = tok_rows // 2
    far_first, far_second = flip(far[:half], 2, 8), flip(far[half:], 4, 8)
    beside = [from_x, flip(from_x, 1, 8), from_y, flip(from_y, 1, 8)]
    side_same, side_other = run(1, 3, beside, 16, far)
    side = [part.astype(F32) for part in (side_same, flip(after(side_other, far_first, far_second), 1, 8))]
    side = side[0] + side[1]
    to_x = jnp.concatenate([side[0, :half], side[0, half:] + far_second.astype(F32)], axis=0).astype(BF16)
    to_y = jnp.concatenate([side[1, :half] + far_first.astype(F32), side[1, half:]], axis=0).astype(BF16)
    terms = [near_same[0], flip(near_other, 1, 8)[0], flip(to_x, 2, 8), flip(to_y, 4, 8)]
    return residual, terms, cache


def on_any_mesh(
    hidden_in, tree_queries, tree_keys, tree_values, parents, accepted, tree_parents, request_prompt, prompt_lengths,
    prompt_keys, prompt_values, out_proj, gain, expert_ids, gate_weights, gate_up, down,
):
    tok_rows, features = hidden_in.shape
    prompt_count, rows_here, _ = prompt_keys.shape
    ep_size = lax.axis_size("ep")
    me = lax.axis_index("ep").astype(jnp.int32)
    keys = lax.all_gather(prompt_keys, "ep", axis=1, tiled=True).reshape(-1, features)
    values = lax.all_gather(prompt_values, "ep", axis=1, tiled=True).reshape(-1, features)
    column = jnp.arange(keys.shape[0], dtype=jnp.int32)
    columns = jnp.stack([column // (rows_here * ep_size), column % (rows_here * ep_size)])
    attended, cache = plain_attention(
        request_prompt, prompt_lengths, columns, parents, accepted, tree_queries, tree_keys, tree_values, keys, values
    )
    joined = lax.all_gather(out_proj, "rep", axis=0, tiled=True)
    projected = jnp.dot(attended, joined, preferred_element_type=F32)
    residual, normed = norm(hidden_in, projected, jnp.zeros(hidden_in.shape, BF16), gain)
    routing = jnp.concatenate([expert_ids.astype(F32).T, gate_weights.T], axis=0)
    routing = lax.all_gather(routing, "ep", axis=0).reshape(ep_size // 2, 2, -1, tok_rows)
    routing = jnp.concatenate([routing[:, 0], routing[:, 1]], axis=-1)
    top = expert_ids.shape[1]
    everyone = lax.all_gather(normed, "ep", axis=0, tiled=True)
    sources = [everyone[i * 2 * tok_rows : (i + 1) * 2 * tok_rows] for i in range(ep_size // 2)]
    slots = route((me * gate_up.shape[0]).reshape(1), routing[:, :top], routing[:, top:], gate_up.shape[0])
    same_core, other_core = experts(
        *slots, list(gate_up), list(down), sources,
        VMEM_LIMIT
    )
    shares = jnp.stack([same_core, other_core], axis=1).reshape(ep_size, tok_rows, features)
    shares = lax.all_to_all(shares, "ep", split_axis=0, concat_axis=0, tiled=True)
    return residual, [shares[i] for i in range(ep_size)], cache


def per_device(
    hidden_in,
    tree_queries,
    tree_keys,
    tree_values,
    tree_parents,
    accepted_nodes,
    request_prompt,
    prompt_lengths,
    prompt_keys,
    prompt_values,
    out_proj,
    norm_gain,
    expert_ids,
    gate_weights,
    expert_gate_up,
    expert_down,
):
    tok_rows, features = hidden_in.shape
    req_count, tree_len = tree_parents.shape
    first_node = jnp.arange(req_count, dtype=jnp.int32)[:, None] * tree_len
    accepted = (first_node + accepted_nodes).reshape(-1, 1)
    parents = jnp.where(tree_parents < 0, -1, tree_parents + first_node).reshape(-1, 1)
    planes = lax.axis_size("ep") == 8 and lax.axis_size("rep") == 4 and out_proj.shape[0] == 4 * HEAD_DIM
    plan = on_planes if planes else on_any_mesh
    residual, terms, cache = plan(
        hidden_in, tree_queries, tree_keys, tree_values, parents, accepted, tree_parents, request_prompt,
        prompt_lengths, prompt_keys, prompt_values, out_proj, norm_gain.reshape(1, features), expert_ids,
        gate_weights, expert_gate_up, expert_down,
    )
    layer_out = residual
    for term in terms:
        layer_out = layer_out + term.astype(F32)
    accepted_cache = cache.reshape(req_count, accepted_nodes.shape[1], 2 * features)
    return (layer_out.astype(BF16), accepted_cache)


def solution(mesh):
    in_specs = (
        P(("rep", "ep"), None),
        P(("rep", "ep"), None),
        P(("rep", "ep"), None),
        P(("rep", "ep"), None),
        P(("rep", "ep"), None),
        P(("rep", "ep"), None),
        P(("rep", "ep")),
        P("rep"),
        P("rep", "ep", None),
        P("rep", "ep", None),
        P("rep", None),
        P(),
        P(("rep", "ep"), None),
        P(("rep", "ep"), None),
        P("ep", None, None),
        P("ep", None, None),
    )
    out_specs = (P(("rep", "ep"), None), P(("rep", "ep"), None, None))
    return jax.shard_map(
        per_device, mesh=mesh, in_specs=in_specs, out_specs=out_specs, check_vma=False
    )
```

```python
import math

import jax
import jax.numpy as jnp
from jax import lax
from jax.experimental import pallas as pl
from jax.experimental.pallas import tpu as pltpu
from jax.sharding import PartitionSpec as P

HEADS = 16
HEAD_DIM = 128
CAP = 40

NEG_FILL = -1e30
EPSILON = 1e-05
VMEM_LIMIT = 56 * 1024 * 1024

F32 = jnp.float32
BF16 = jnp.bfloat16


def flip(value, bits, size):
    return lax.ppermute(value, "ep", [(i, i ^ bits) for i in range(size)])


def in_hbm(value):
    return pltpu.with_memory_space_constraint(value, pltpu.HBM)


def in_vmem(value):
    return pltpu.with_memory_space_constraint(value, pltpu.VMEM)


def after(value, *done):
    return lax.optimization_barrier((value, done))[0]


def everywhere(shape, dtype):
    return jax.ShapeDtypeStruct(shape, dtype)


IN_VMEM = pl.BlockSpec(memory_space=pltpu.VMEM)
IN_SMEM = pl.BlockSpec(memory_space=pltpu.SMEM)
IN_PLACE = pl.BlockSpec(memory_space=pl.ANY)


def pack_body(place, *refs):
    sources, out_proj, (send, send_prompts, prompts, block) = refs[:7], refs[7], refs[8:12]
    held, sems = refs[12:19], refs[19]
    core, parity = place[0] % 2, (place[0] // 2 + place[0] // 4) % 2
    head_rows = pl.ds(pl.multiple_of((2 * core + parity) * HEAD_DIM, HEAD_DIM), HEAD_DIM)
    copies = [pltpu.make_async_copy(sources[i], held[i], sems.at[i]) for i in range(7)]
    copies.append(pltpu.make_async_copy(out_proj.at[head_rows], block, sems.at[7]))
    for copy in copies:
        copy.start()
    for copy in copies:
        copy.wait()
    queries, keys, values, prompt_keys, prompt_values, ids, gates = held
    rows, features = queries.shape
    shards = features // (4 * HEAD_DIM)
    width = 2 * HEAD_DIM
    for shard in range(shards):
        lanes = slice(shard * width, (shard + 1) * width)
        for target, which in ((0, core), (1, 1 - core)):
            start = pl.multiple_of(shard * 2 * width + which * width, width)
            low = 0
            for part in (queries, keys, values, prompt_keys, prompt_values):
                high = low + part.shape[0]
                if high > 3 * rows:
                    kept = slice(low - 3 * rows, high - 3 * rows)
                    (prompts, send_prompts)[target][kept, lanes] = part[:, pl.ds(start, width)]
                elif target == 1:
                    send[low:high, lanes] = part[:, pl.ds(start, width)]
                low = high
    top = ids.shape[0]
    high_part = gates[...].astype(BF16)
    low_part = (gates[...] - high_part.astype(F32)).astype(BF16)
    blank = jnp.zeros((top, rows), F32)
    first = jnp.concatenate([ids[...].astype(F32), high_part.astype(F32)], axis=0).astype(BF16)
    second = jnp.concatenate([blank, low_part.astype(F32)], axis=0).astype(BF16)
    base = 2 * prompt_keys.shape[0]
    for target in (send_prompts, prompts):
        target[base : base + 2 * top, :] = jnp.zeros((2 * top, target.shape[1]), BF16)
        target[base : base + 2 * top, :rows] = first
        target[base : base + 2 * top, rows : 2 * rows] = second


def pack(place, queries, keys, values, prompt_keys, prompt_values, ids, gates, out_proj):
    rows, features = queries.shape
    tail = 2 * prompt_keys.shape[0] + 2 * ids.shape[0]
    parts = (queries, keys, values, prompt_keys, prompt_values, ids, gates)
    return pl.pallas_call(
        pack_body,
        out_shape=(
            everywhere((3 * rows, features // 2), BF16),
            everywhere((tail, features // 2), BF16),
            everywhere((tail, features // 2), BF16),
            everywhere((HEAD_DIM, features), BF16),
        ),
        in_specs=[IN_SMEM] + [IN_PLACE] * 8,
        out_specs=(IN_VMEM,) * 4,
        scratch_shapes=[pltpu.VMEM(part.shape, part.dtype) for part in parts] + [pltpu.SemaphoreType.DMA((8,))],
        compiler_params=pltpu.CompilerParams(vmem_limit_bytes=12 * 2**20),
        name="pack",
    )(place, *[in_hbm(part) for part in (*parts, out_proj)])


def attend(queries, all_keys, all_values, bias):
    scores = lax.dot_general(queries, all_keys, (((1,), (1,)), ((), ())), preferred_element_type=F32)
    scores = scores * (1.0 / math.sqrt(HEAD_DIM)) + bias
    weights = jnp.exp(scores - jnp.max(scores, axis=-1, keepdims=True))
    total = jnp.sum(weights, axis=-1, keepdims=True)
    mixed = jnp.dot(weights.astype(BF16), all_values, preferred_element_type=F32)
    return (mixed / total).astype(BF16)


def fill_bias(bias, prompt_rows, tree_len, parents, prompts, lengths, prompt_of, position):
    tokens = bias.shape[0]
    for request in range(tokens // tree_len):
        prompt = prompts[request]
        seen = (prompt_of == prompt) & (position < lengths[prompt])
        row = jnp.where(seen, 0.0, NEG_FILL)
        bias[request * tree_len : (request + 1) * tree_len, :prompt_rows] = jnp.broadcast_to(
            row, (tree_len, prompt_rows)
        )
    node = lax.broadcasted_iota(jnp.int32, (tokens, tokens), 0)
    other = lax.broadcasted_iota(jnp.int32, (tokens, tokens), 1)
    reach = jnp.where((other == parents) | (other == node), 1.0, 0.0)
    for _ in range((tree_len - 1).bit_length()):
        reach = reach.astype(BF16)
        reach = jnp.minimum(jnp.dot(reach, reach, preferred_element_type=F32), 1.0)
    bias[:, prompt_rows:] = jnp.where(reach > 0.5, 0.0, NEG_FILL)


def accepted_body(accepted, tree_keys, tree_values, cache):
    rows, features = tree_keys.shape
    chosen = accepted[...] == lax.broadcasted_iota(jnp.int32, (accepted.shape[0], rows), 1)
    chosen = jnp.where(chosen, 1.0, 0.0).astype(BF16)
    cache[:, :features] = jnp.dot(chosen, tree_keys[...], preferred_element_type=F32).astype(BF16)
    cache[:, features:] = jnp.dot(chosen, tree_values[...], preferred_element_type=F32).astype(BF16)


def chip_attention_body(
    me, my_prompts, sibling, lengths, columns, parents, accepted, prompts_here, got, *refs
):
    copies = [pltpu.make_async_copy(refs[i], refs[15 + i], refs[25].at[i]) for i in range(10)]
    for copy in copies:
        copy.start()
    (attended, cache, ids, gates, bias), (queries_here, tree_keys, tree_values, *holders) = refs[10:15], refs[15:25]
    holders = [prompts_here, *holders]
    rows = tree_keys.shape[0]
    requests = my_prompts.shape[0]
    tree_len = rows // requests
    block = (holders[0].shape[0] - 16) // 2
    prompts = [my_prompts[i] for i in range(requests)] + [sibling[requests + i, 0] for i in range(requests)]
    position = (columns[0:1, :] ^ me[0]) * (block // lengths.shape[0]) + columns[2:3, :]
    fill_bias(bias, columns.shape[1], tree_len, parents[...], prompts, lengths, columns[1:2, :], position)
    for copy in copies:
        copy.wait()
    for head in range(got.shape[1] // HEAD_DIM):
        lanes = slice(head * HEAD_DIM, (head + 1) * HEAD_DIM)
        place = head // 2 * 4 * HEAD_DIM + me[0] % 2 * 2 * HEAD_DIM + head % 2 * HEAD_DIM
        mine = pl.ds(pl.multiple_of(place, HEAD_DIM), HEAD_DIM)
        queries = jnp.concatenate([queries_here[:, mine], got[:rows, lanes]], axis=0)
        all_keys = jnp.concatenate(
            [ref[:block, lanes] for ref in holders]
            + [tree_keys[:, mine], got[rows : 2 * rows, lanes]],
            axis=0,
        )
        all_values = jnp.concatenate(
            [ref[block : 2 * block, lanes] for ref in holders]
            + [tree_values[:, mine], got[2 * rows : 3 * rows, lanes]],
            axis=0,
        )
        attended[head] = attend(queries, all_keys, all_values, bias[...])
    accepted_body(accepted, tree_keys, tree_values, cache)
    for index, ref in enumerate(holders):
        first = ref[2 * block :, :rows].astype(F32)
        second = ref[2 * block :, rows : 2 * rows].astype(F32)
        lanes = slice(index % 2 * rows, (index % 2 + 1) * rows)
        ids[index // 2, :, lanes] = first[:8]
        gates[index // 2, :, lanes] = first[8:] + second[8:]


def chip_attention(scalars, columns, parents, accepted, queries, tree_keys, tree_values, prompts, got, blocks):
    rows, features = tree_keys.shape
    width = columns.shape[1] + 2 * rows
    heads = features // HEAD_DIM // 2
    copied = [in_hbm(part) for part in (queries, tree_keys, tree_values, *blocks)]
    return pl.pallas_call(
        chip_attention_body,
        out_shape=(
            everywhere((heads, 2 * rows, HEAD_DIM), BF16),
            everywhere((accepted.shape[0], 2 * features), BF16),
            everywhere((4, 8, 2 * rows), F32),
            everywhere((4, 8, 2 * rows), F32),
        ),
        in_specs=[IN_SMEM] * 4 + [IN_VMEM] * 5 + [IN_PLACE] * len(copied),
        out_specs=(IN_VMEM,) * 4,
        scratch_shapes=[pltpu.VMEM((2 * rows, width), F32)]
        + [pltpu.VMEM(part.shape, BF16) for part in copied]
        + [pltpu.SemaphoreType.DMA((len(copied),))],
        compiler_params=pltpu.CompilerParams(vmem_limit_bytes=14 * 2**20),
        name="attention",
    )(*scalars, columns, parents, accepted, prompts, got, *copied)


def plain_attention_body(
    prompts, lengths, columns, parents, accepted, queries, tree_keys, tree_values, keys, values, attended, cache, bias
):
    rows, features = queries.shape
    tree_len = rows // prompts.shape[0]
    requests = [prompts[i] for i in range(prompts.shape[0])]
    fill_bias(bias, columns.shape[1], tree_len, parents[...], requests, lengths, columns[0:1, :], columns[1:2, :])
    for head in range(features // HEAD_DIM):
        lanes = slice(head * HEAD_DIM, (head + 1) * HEAD_DIM)
        all_keys = jnp.concatenate([keys[:, lanes], tree_keys[:, lanes]], axis=0)
        all_values = jnp.concatenate([values[:, lanes], tree_values[:, lanes]], axis=0)
        attended[:, lanes] = attend(queries[:, lanes], all_keys, all_values, bias[...])
    accepted_body(accepted, tree_keys, tree_values, cache)


def plain_attention(prompts, lengths, columns, parents, accepted, queries, tree_keys, tree_values, keys, values):
    rows, features = queries.shape
    return pl.pallas_call(
        plain_attention_body,
        out_shape=(everywhere((rows, features), BF16), everywhere((accepted.shape[0], 2 * features), BF16)),
        in_specs=[IN_SMEM] * 2 + [IN_VMEM] * 8,
        out_specs=(IN_VMEM,) * 2,
        scratch_shapes=[pltpu.VMEM((rows, columns.shape[1] + rows), F32)],
        compiler_params=pltpu.CompilerParams(vmem_limit_bytes=VMEM_LIMIT),
        name="attention",
    )(prompts, lengths, columns, parents, accepted, queries, tree_keys, tree_values, keys, values)


def weave_body(upper, lower, first, second):
    half = upper.shape[0] // 2
    first[:half, :] = upper[:half, :]
    first[half:, :] = lower[:half, :]
    second[:half, :] = upper[half:, :]
    second[half:, :] = lower[half:, :]


def weave(upper, lower):
    return pl.pallas_call(
        weave_body,
        out_shape=(everywhere(upper.shape, upper.dtype),) * 2,
        in_specs=[IN_VMEM] * 2,
        out_specs=(IN_VMEM,) * 2,
        compiler_params=pltpu.CompilerParams(vmem_limit_bytes=6 * 2**20),
        name="weave",
    )(upper, lower)


def fetch_projection(out_proj, block, before_shared):
    me, place = lax.axis_index("rep"), lax.axis_index("ep")
    core, parity = place % 2, (place // 2 + place // 4) % 2
    own = lax.dynamic_slice_in_dim(out_proj, core * 2 * HEAD_DIM, 2 * HEAD_DIM, 0)

    def shifted(value, by):
        return lax.ppermute(value, "rep", [(i, (i + by) % 4) for i in range(4)])

    came1, came3 = shifted(block, 1), shifted(block, 3)
    up = lax.ppermute(came1, "rep", [(1, 2), (2, 3)])
    down = lax.ppermute(came3, "rep", [(2, 1), (1, 0)])
    order = [2 * me, 2 * me + 1]
    for by in (1, 3, 2):
        shard = (me + 4 - by) % 4
        order += [2 * shard + parity, 2 * shard + 1 - parity]
    half = HEAD_DIM // 2
    came1, came3 = after((came1, came3), before_shared)
    first, second = weave(came1, came3)
    from_x, from_y = flip(first, 2, 8), flip(second, 4, 8)
    weights = [own, first, second, from_x, from_y]
    pieces = [(0, 0, 2 * HEAD_DIM)]
    for low in (0, half):
        pieces += [(index, low, low + half) for index in (1, 2, 3, 4)]
    pieces += [(index, 0, half) for index in (5, 6, 7, 8)]
    return weights, pieces, jnp.stack(order).astype(jnp.int32), up, down


def chip_project_body(pieces, low_row, order, attended, *refs):
    weights, (result, ordered) = refs[: len(refs) - 2], refs[len(refs) - 2 :]
    rows, features = result.shape
    for index in range(attended.shape[0]):
        ordered[:, index * HEAD_DIM : (index + 1) * HEAD_DIM] = attended[order[index], low_row : low_row + rows, :]
    step = 256
    for column in range(0, features, step):
        joined = jnp.concatenate(
            [weights[ref][low:high, column : column + step] for ref, low, high in pieces], axis=0
        )
        total = jnp.dot(ordered[...], joined, preferred_element_type=F32)
        result[:, column : column + step] = total.astype(result.dtype)


def chip_project(order, attended, weights, pieces, low_row, dtype):
    heads, rows, _ = attended.shape
    features = weights[0].shape[1]
    return pl.pallas_call(
        lambda *refs: chip_project_body(pieces, low_row, *refs),
        out_shape=everywhere((rows // 2, features), dtype),
        in_specs=[IN_SMEM] + [IN_VMEM] * (1 + len(weights)),
        out_specs=IN_VMEM,
        scratch_shapes=[pltpu.VMEM((rows // 2, heads * HEAD_DIM), BF16)],
        compiler_params=pltpu.CompilerParams(vmem_limit_bytes=14 * 2**20),
        name="project",
    )(order, attended, *weights)


def norm_body(hidden, mine, other, gain, residual, normed):
    total = hidden[...].astype(F32) + mine[...] + other[...].astype(F32)
    residual[...] = total
    factor = lax.rsqrt(jnp.mean(total * total, axis=-1, keepdims=True) + EPSILON)
    normed[...] = (total * factor * gain[...]).astype(BF16)


def norm(hidden, mine, other, gain):
    return pl.pallas_call(
        norm_body,
        out_shape=(everywhere(hidden.shape, F32), everywhere(hidden.shape, BF16)),
        in_specs=[IN_VMEM] * 4,
        out_specs=(IN_VMEM,) * 2,
        compiler_params=pltpu.CompilerParams(vmem_limit_bytes=8 * 2**20),
        name="norm",
    )(hidden, mine, other, gain)


def stage_body(gate_up, down, *refs):
    count = gate_up.shape[0]
    sems = refs[2 * count]
    copies = []
    for expert in range(count):
        copies.append(pltpu.make_async_copy(gate_up.at[expert], refs[expert], sems.at[expert]))
        copies.append(pltpu.make_async_copy(down.at[expert], refs[count + expert], sems.at[count + expert]))
    for copy in copies:
        copy.start()
    for copy in copies:
        copy.wait()


def stage(gate_up, down):
    count = gate_up.shape[0]
    staged = pl.pallas_call(
        stage_body,
        out_shape=[pltpu.VMEM(gate_up.shape[1:], BF16)] * count + [pltpu.VMEM(down.shape[1:], BF16)] * count,
        in_specs=[IN_PLACE] * 2,
        out_specs=[IN_PLACE] * (2 * count),
        scratch_shapes=[pltpu.SemaphoreType.DMA((2 * count,))],
        compiler_params=pltpu.CompilerParams(vmem_limit_bytes=2**20),
        cost_estimate=pl.CostEstimate(flops=0, bytes_accessed=2 * (gate_up.size + down.size), transcendentals=0),
        name="stage",
    )(in_hbm(gate_up), in_hbm(down))
    return staged[:count], staged[count:]


def route_body(local_experts, first_expert, ids, gates, chosen, slot_gates):
    pairs, top, tokens = ids.shape
    slots = 2 * CAP
    earlier = lax.broadcasted_iota(jnp.int32, (tokens, tokens), 0)
    later = lax.broadcasted_iota(jnp.int32, (tokens, tokens), 1)
    before = jnp.where(earlier < later, 1.0, 0.0).astype(BF16)
    slot_ids = lax.broadcasted_iota(jnp.int32, (slots, tokens), 0).astype(F32)
    for pair in range(pairs):
        hits, shares = [], []
        for expert in range(local_experts):
            match = ids[pair] == (first_expert[0] + expert).astype(F32)
            hits.append(jnp.max(jnp.where(match, 1.0, 0.0), axis=0, keepdims=True))
            shares.append(jnp.sum(jnp.where(match, gates[pair], 0.0), axis=0, keepdims=True))
        stacked = jnp.concatenate(hits + [jnp.zeros((16 - local_experts, tokens), F32)], axis=0)
        places = jnp.dot(stacked.astype(BF16), before, preferred_element_type=F32)
        for expert in range(local_experts):
            place = jnp.where(hits[expert] > 0.5, places[expert : expert + 1], -1.0)
            taken = jnp.where(slot_ids == place, 1.0, 0.0)
            rows = slice(expert * slots, (expert + 1) * slots)
            chosen[pair, rows, :] = taken.astype(BF16)
            slot_gates[pair, rows, :] = jnp.sum(taken * shares[expert], axis=1, keepdims=True)


def route(first_expert, ids, gates, local_experts):
    pairs, top, tokens = ids.shape
    rows = local_experts * 2 * CAP
    return pl.pallas_call(
        lambda *refs: route_body(local_experts, *refs),
        out_shape=(everywhere((pairs, rows, tokens), BF16), everywhere((pairs, rows, 1), F32)),
        in_specs=[IN_SMEM, IN_VMEM, IN_VMEM],
        out_specs=(IN_VMEM,) * 2,
        compiler_params=pltpu.CompilerParams(vmem_limit_bytes=24 * 2**20),
        name="route",
    )(first_expert, ids, gates)


def experts_body(per_pair, local_experts, chosen, slot_gates, *refs):
    pairs, _, tokens = chosen.shape
    gate_up, down, refs = refs[:local_experts], refs[local_experts : 2 * local_experts], refs[2 * local_experts :]
    sources = refs[: pairs * per_pair]
    same_core, other_core, picked, produced, hidden = refs[pairs * per_pair :]
    features, units = gate_up[0].shape[0], down[0].shape[0]
    slots = 2 * CAP
    for pair in range(pairs):
        group = sources[pair * per_pair : (pair + 1) * per_pair]
        step = 512
        for column in range(0, features, step):
            rows = jnp.concatenate([ref[:, column : column + step] for ref in group], axis=0)
            found = jnp.dot(chosen[pair], rows, preferred_element_type=F32).astype(BF16)
            for expert in range(local_experts):
                picked[expert, pair * slots : (pair + 1) * slots, column : column + step] = found[
                    expert * slots : (expert + 1) * slots
                ]
    chunk = slots * min(pairs, 4)
    for expert in range(local_experts):
        for low in range(0, pairs * slots, chunk):
            rows = picked[expert, low : low + chunk, :]
            gate_rows = jnp.concatenate(
                [
                    slot_gates[low // slots + inner, expert * slots : (expert + 1) * slots, :]
                    for inner in range(chunk // slots)
                ],
                axis=0,
            )
            for column in range(0, units, 256):
                gate = jnp.dot(rows, gate_up[expert][:, column : column + 256], preferred_element_type=F32)
                up = jnp.dot(
                    rows, gate_up[expert][:, units + column : units + column + 256], preferred_element_type=F32
                )
                active = gate / (1.0 + jnp.exp(-gate)) * up * gate_rows
                hidden[low : low + chunk, column : column + 256] = active.astype(BF16)
            for column in range(0, features, 512):
                result = jnp.dot(
                    hidden[low : low + chunk, :], down[expert][:, column : column + 512], preferred_element_type=F32
                ).astype(BF16)
                for inner in range(chunk // slots):
                    produced[
                        low // slots + inner, expert * slots : (expert + 1) * slots, column : column + 512
                    ] = result[inner * slots : (inner + 1) * slots]
    for pair in range(pairs):
        for column in range(0, features, 512):
            mixture = lax.dot_general(
                chosen[pair], produced[pair, :, column : column + 512], (((0,), (0,)), ((), ())),
                preferred_element_type=F32,
            ).astype(BF16)
            same_core[pair, :, column : column + 512] = mixture[: tokens // 2]
            other_core[pair, :, column : column + 512] = mixture[tokens // 2 :]


def experts(chosen, slot_gates, gate_up, down, sources, limit, pin=False):
    pairs, _, tokens = chosen.shape
    local_experts, (features, _) = len(gate_up), gate_up[0].shape
    units = down[0].shape[0]
    slots = 2 * CAP
    matrices = [*gate_up, *down]
    if pin:
        matrices = [in_vmem(part) for part in matrices]
    return pl.pallas_call(
        lambda *refs: experts_body(len(sources) // pairs, local_experts, *refs),
        out_shape=(everywhere((pairs, tokens // 2, features), BF16),) * 2,
        in_specs=[IN_VMEM] * (2 + 2 * local_experts + len(sources)),
        out_specs=(IN_VMEM,) * 2,
        scratch_shapes=[
            pltpu.VMEM((local_experts, pairs * slots, features), BF16),
            pltpu.VMEM((pairs, local_experts * slots, features), BF16),
            pltpu.VMEM((pairs * slots, units), BF16),
        ],
        compiler_params=pltpu.CompilerParams(vmem_limit_bytes=limit),
        cost_estimate=pl.CostEstimate(
            flops=12 * local_experts * pairs * slots * features * units, bytes_accessed=16 * 2**20, transcendentals=0
        ),
        name="experts",
    )(chosen, slot_gates, *matrices, *sources)


def add_rows(left, right):
    return (left.astype(F32) + right.astype(F32)).astype(BF16)


def on_planes(
    hidden_in, tree_queries, tree_keys, tree_values, parents, accepted, tree_parents, request_prompt, prompt_lengths,
    prompt_keys, prompt_values, out_proj, gain, expert_ids, gate_weights, gate_up, down,
):
    tok_rows, features = hidden_in.shape
    prompt_count, rows_here, _ = prompt_keys.shape
    me = lax.axis_index("ep").astype(jnp.int32)

    flat = (prompt_count * rows_here, features)
    send, send_prompts, prompts, block = pack(
        me.reshape(1), tree_queries, tree_keys, tree_values, prompt_keys.reshape(flat),
        prompt_values.reshape(flat), expert_ids.T, gate_weights.T, out_proj,
    )
    x_mine, y_mine = flip(prompts, 2, 8), flip(prompts, 4, 8)
    theirs = flip(send_prompts, 1, 8)
    x_theirs, y_theirs = flip(theirs, 2, 8), flip(theirs, 4, 8)
    far_a, far_b = flip(x_mine, 4, 8), flip(y_theirs, 2, 8)
    weights, pieces, order, up, down_rows = fetch_projection(out_proj, block, (x_mine, y_mine, x_theirs, y_theirs, far_a, far_b))
    got = flip(send, 1, 8)
    small = jnp.concatenate(
        [tree_parents, jnp.broadcast_to(request_prompt[:, None], tree_parents.shape)], axis=0
    )
    sibling = flip(after(small, x_mine), 1, 8)

    column = jnp.arange(8 * flat[0], dtype=jnp.int32)
    columns = jnp.stack([column // flat[0], column % flat[0] // rows_here, column % rows_here])
    chip_parents = jnp.concatenate([tree_parents, sibling[: tree_parents.shape[0]]], axis=0)
    first_node = jnp.arange(chip_parents.shape[0], dtype=jnp.int32)[:, None] * tree_parents.shape[1]
    chip_parents = jnp.where(chip_parents < 0, -1, chip_parents + first_node).reshape(-1, 1)
    attended, cache, ids, gates = chip_attention(
        (me.reshape(1), request_prompt, sibling, prompt_lengths), columns, chip_parents, accepted,
        tree_queries, tree_keys, tree_values, prompts, got, (theirs, x_mine, x_theirs, y_mine, y_theirs, far_a, far_b),
    )
    up, down_rows = after((up, down_rows), attended)
    edge = up.shape[0] // 2
    last_first, last_second = [
        jnp.where(lax.axis_index("rep") >= 2, up[rows], down_rows[rows]) for rows in (slice(0, edge), slice(edge, None))
    ]
    weights += [last_first, last_second, flip(last_first, 2, 8), flip(last_second, 4, 8)]
    chosen, slot_gates = route((me * gate_up.shape[0]).reshape(1), after(ids, last_first), gates, gate_up.shape[0])
    attended = after(attended, chosen)
    other = flip(chip_project(order, attended, weights, pieces, tok_rows, BF16), 1, 8)
    mine = chip_project(order, attended, weights, pieces, 0, F32)
    residual, normed = norm(hidden_in, mine, other, gain)

    across, from_x, from_y = flip(normed, 6, 8), flip(normed, 2, 8), flip(normed, 4, 8)
    sibling_rows = flip(normed, 1, 8)
    gate_up, down = stage(*after((gate_up, down), normed))

    def run(low, high, sources, megabytes, *done):
        return experts(
            after(chosen[low:high], done), slot_gates[low:high], gate_up, down, sources, megabytes * 2**20, True
        )

    near_same, near_other = run(0, 1, [normed, sibling_rows], 12)
    across = after(across, near_same)
    far_same, far_other = run(3, 4, [across, flip(across, 1, 8)], 12)
    far = add_rows(far_same, flip(far_other, 1, 8))[0]

    half = tok_rows // 2
    far_first, far_second = flip(far[:half], 2, 8), flip(far[half:], 4, 8)
    beside = [from_x, flip(from_x, 1, 8), from_y, flip(from_y, 1, 8)]
    side_same, side_other = run(1, 3, beside, 16, far)
    side = [part.astype(F32) for part in (side_same, flip(after(side_other, far_first, far_second), 1, 8))]
    side = side[0] + side[1]
    to_x = jnp.concatenate([side[0, :half], side[0, half:] + far_second.astype(F32)], axis=0).astype(BF16)
    to_y = jnp.concatenate([side[1, :half] + far_first.astype(F32), side[1, half:]], axis=0).astype(BF16)
    terms = [near_same[0], flip(near_other, 1, 8)[0], flip(to_x, 2, 8), flip(to_y, 4, 8)]
    return residual, terms, cache


def on_any_mesh(
    hidden_in, tree_queries, tree_keys, tree_values, parents, accepted, tree_parents, request_prompt, prompt_lengths,
    prompt_keys, prompt_values, out_proj, gain, expert_ids, gate_weights, gate_up, down,
):
    tok_rows, features = hidden_in.shape
    prompt_count, rows_here, _ = prompt_keys.shape
    ep_size = lax.axis_size("ep")
    me = lax.axis_index("ep").astype(jnp.int32)
    keys = lax.all_gather(prompt_keys, "ep", axis=1, tiled=True).reshape(-1, features)
    values = lax.all_gather(prompt_values, "ep", axis=1, tiled=True).reshape(-1, features)
    column = jnp.arange(keys.shape[0], dtype=jnp.int32)
    columns = jnp.stack([column // (rows_here * ep_size), column % (rows_here * ep_size)])
    attended, cache = plain_attention(
        request_prompt, prompt_lengths, columns, parents, accepted, tree_queries, tree_keys, tree_values, keys, values
    )
    joined = lax.all_gather(out_proj, "rep", axis=0, tiled=True)
    projected = jnp.dot(attended, joined, preferred_element_type=F32)
    residual, normed = norm(hidden_in, projected, jnp.zeros(hidden_in.shape, BF16), gain)
    routing = jnp.concatenate([expert_ids.astype(F32).T, gate_weights.T], axis=0)
    routing = lax.all_gather(routing, "ep", axis=0).reshape(ep_size // 2, 2, -1, tok_rows)
    routing = jnp.concatenate([routing[:, 0], routing[:, 1]], axis=-1)
    top = expert_ids.shape[1]
    everyone = lax.all_gather(normed, "ep", axis=0, tiled=True)
    sources = [everyone[i * 2 * tok_rows : (i + 1) * 2 * tok_rows] for i in range(ep_size // 2)]
    slots = route((me * gate_up.shape[0]).reshape(1), routing[:, :top], routing[:, top:], gate_up.shape[0])
    same_core, other_core = experts(
        *slots, list(gate_up), list(down), sources,
        VMEM_LIMIT
    )
    shares = jnp.stack([same_core, other_core], axis=1).reshape(ep_size, tok_rows, features)
    shares = lax.all_to_all(shares, "ep", split_axis=0, concat_axis=0, tiled=True)
    return residual, [shares[i] for i in range(ep_size)], cache


def per_device(
    hidden_in,
    tree_queries,
    tree_keys,
    tree_values,
    tree_parents,
    accepted_nodes,
    request_prompt,
    prompt_lengths,
    prompt_keys,
    prompt_values,
    out_proj,
    norm_gain,
    expert_ids,
    gate_weights,
    expert_gate_up,
    expert_down,
):
    tok_rows, features = hidden_in.shape
    req_count, tree_len = tree_parents.shape
    first_node = jnp.arange(req_count, dtype=jnp.int32)[:, None] * tree_len
    accepted = (first_node + accepted_nodes).reshape(-1, 1)
    parents = jnp.where(tree_parents < 0, -1, tree_parents + first_node).reshape(-1, 1)
    planes = lax.axis_size("ep") == 8 and lax.axis_size("rep") == 4 and out_proj.shape[0] == 4 * HEAD_DIM
    plan = on_planes if planes else on_any_mesh
    residual, terms, cache = plan(
        hidden_in, tree_queries, tree_keys, tree_values, parents, accepted, tree_parents, request_prompt,
        prompt_lengths, prompt_keys, prompt_values, out_proj, norm_gain.reshape(1, features), expert_ids,
        gate_weights, expert_gate_up, expert_down,
    )
    layer_out = residual
    for term in terms:
        layer_out = layer_out + term.astype(F32)
    accepted_cache = cache.reshape(req_count, accepted_nodes.shape[1], 2 * features)
    return (layer_out.astype(BF16), accepted_cache)


def solution(mesh):
    in_specs = (
        P(("rep", "ep"), None),
        P(("rep", "ep"), None),
        P(("rep", "ep"), None),
        P(("rep", "ep"), None),
        P(("rep", "ep"), None),
        P(("rep", "ep"), None),
        P(("rep", "ep")),
        P("rep"),
        P("rep", "ep", None),
        P("rep", "ep", None),
        P("rep", None),
        P(),
        P(("rep", "ep"), None),
        P(("rep", "ep"), None),
        P("ep", None, None),
        P("ep", None, None),
    )
    out_specs = (P(("rep", "ep"), None), P(("rep", "ep"), None, None))
    return jax.shard_map(
        per_device, mesh=mesh, in_specs=in_specs, out_specs=out_specs, check_vma=False
    )
```
